512 devices in a mesh: dap: 32 (over z, x_lo), pair: 16 (over y, x_hi, core).
Axes of the slice: x: 4 (x_hi: 2, x_lo: 2; x = x_hi * 2 + x_lo), y: 4, z: 16, core: 2. Of those that a mesh axis runs over, the one named last changes fastest.
Arguments:
- alignment_activity: bfloat16 [128, 512, 256], P('pair', 'dap'), may hold values from -6 to 6
- existing_strand_flags: int32 [128], replicated, may hold values from 0 to 1
- existing_position_flags: int32 [512], replicated, may hold values 0 or 1
- asking_vector_map: bfloat16 [256, 256], replicated, may hold values from -2.2 to 2.2
- lookup_address_map: bfloat16 [256, 256], replicated, may hold values from -2.2 to 2.2
- content_vector_map: bfloat16 [256, 256], replicated, may hold values from -0.375 to 0.375
- sigmoid_switch_map: bfloat16 [256, 256], replicated, may hold values from -0.375 to 0.375
- final_mixing_map: bfloat16 [256, 256], replicated, may hold values from -0.375 to 0.375
- final_offset_vector: float32 [256], replicated, may hold values from -3 to 3
- first_factor_map: bfloat16 [256, 32], replicated, may hold values from -0.375 to 0.375
- first_factor_offset: float32 [32], replicated, may hold values from -3 to 3
- second_factor_map: bfloat16 [256, 32], replicated, may hold values from -0.375 to 0.375
- second_factor_offset: float32 [32], replicated, may hold values from -3 to 3
- couple_mixing_map: bfloat16 [1024, 128], replicated, may hold values from -1 to 1
- couple_change_offset: float32 [128], replicated, may hold values from -3 to 3
Outputs:
- vertical_change: bfloat16 [128, 512, 256], P('pair', 'dap')
- pair_update: bfloat16 [512, 512, 128], P('dap', 'pair')
The draws below stay inside these ranges and needn't reach their ends.
All inputs are finite; a program needn't handle non-finite values.
Results may differ from the reference program's by a relative error of at most 0.015.
Values may be sent and summed in bfloat16 or wider, within the bound.
A program may use at most 128 MiB of HBM per device.

```python
import jax
import jax.numpy as jnp
from jax import lax

ALIGN_DEPTH = 256
C_Z = 128
HEADS = 8
HEAD_SIZE = 32
OUTER_FACTORS = 32
ALIGNED_STRANDS = 128
CHAIN_LENGTH = 512
N_DAP = 32


def draw_asking_vector_map(key, part):
    key = jax.random.fold_in(key, 1)
    return (jnp.clip(jax.random.normal(key, (ALIGN_DEPTH, ALIGN_DEPTH), jnp.float32), -4.0, 4.0) * (2.0 / ALIGN_DEPTH) ** 0.5).astype(jnp.bfloat16)


def draw_lookup_address_map(key, part):
    key = jax.random.fold_in(key, 2)
    return (jnp.clip(jax.random.normal(key, (ALIGN_DEPTH, ALIGN_DEPTH), jnp.float32), -4.0, 4.0) * (2.0 / ALIGN_DEPTH) ** 0.5).astype(jnp.bfloat16)


def draw_existing_strand_flags(key, part):
    key = jax.random.fold_in(key, 3)
    tickets = jax.random.randint(key, (ALIGNED_STRANDS,), 0, 1000, dtype=jnp.int32)
    limits = 950 - 650 * jnp.arange(ALIGNED_STRANDS, dtype=jnp.int32) // ALIGNED_STRANDS
    kept = (tickets < limits).astype(jnp.int32)
    return kept.at[0].set(1)


def set_ends(result, own_key, least, top_value):
    extent = result.shape
    index_at = [jax.random.randint(jax.random.fold_in(own_key, axis), (), 0, extent[axis]) for axis in range(len(extent))]
    result = result.at[tuple(index_at)].set(least)
    longest = extent.index(max(extent))
    index_at[longest] = (index_at[longest] + 1) % extent[longest]
    return result.at[tuple(index_at)].set(top_value)


def levels(stream_key, shape, cuts, low, largest):
    factor_of = 1.0
    for position, parts in cuts:
        draws = jax.random.uniform(jax.random.fold_in(jax.random.fold_in(stream_key, 6), position), (parts,), jnp.float32, low / len(cuts), largest / len(cuts))
        factor_of = factor_of * jnp.repeat(jnp.exp(draws), shape[position] // parts).reshape((-1,) + (1,) * (len(shape) - 1 - position))
    return factor_of


def noise(own_key, dims, width, reach, cuts=(), kind=jnp.bfloat16):
    values = jax.random.normal(own_key, dims, jnp.float32) * width
    if len(cuts) > 0:
        values = levels(own_key, dims, cuts, -0.22, 0.18) * values
    return jnp.clip(values, min=-reach, max=reach).astype(kind)


def setup_inputs(seed: int = 0) -> dict:
    splits = jax.random.split(jax.random.key(seed), 16)
    alignment_activity = noise(splits[0], (ALIGNED_STRANDS, CHAIN_LENGTH, ALIGN_DEPTH), 1.0, 6.0, ((0, 16), (1, 32)))
    existing_strand_flags = draw_existing_strand_flags(jax.random.fold_in(splits[15], 71), 0)
    existing_position_flags = set_ends((jax.random.randint(splits[2], (CHAIN_LENGTH,), 0, 8) < 7).astype(jnp.int32), jax.random.fold_in(splits[2], 1), 0, 1)
    asking_vector_map = draw_asking_vector_map(jax.random.fold_in(splits[15], 71), 0)
    lookup_address_map = draw_lookup_address_map(jax.random.fold_in(splits[15], 71), 0)
    content_vector_map = noise(splits[5], (ALIGN_DEPTH, ALIGN_DEPTH), ALIGN_DEPTH ** -0.5, 0.375)
    sigmoid_switch_map = noise(splits[6], (ALIGN_DEPTH, ALIGN_DEPTH), ALIGN_DEPTH ** -0.5, 0.375)
    final_mixing_map = noise(splits[7], (ALIGN_DEPTH, ALIGN_DEPTH), ALIGN_DEPTH ** -0.5, 0.375)
    final_offset_vector = noise(splits[8], (ALIGN_DEPTH,), 0.5, 3.0, (), jnp.float32)
    first_factor_map = noise(splits[9], (ALIGN_DEPTH, OUTER_FACTORS), ALIGN_DEPTH ** -0.5, 0.375)
    first_factor_offset = noise(splits[10], (OUTER_FACTORS,), 0.5, 3.0, (), jnp.float32)
    second_factor_map = noise(splits[11], (ALIGN_DEPTH, OUTER_FACTORS), ALIGN_DEPTH ** -0.5, 0.375)
    second_factor_offset = noise(splits[12], (OUTER_FACTORS,), 0.5, 3.0, (), jnp.float32)
    couple_mixing_map = noise(splits[13], (OUTER_FACTORS * OUTER_FACTORS, C_Z), OUTER_FACTORS ** -0.5, 1.0)
    couple_change_offset = noise(splits[14], (C_Z,), 0.5, 3.0, (), jnp.float32)
    return {"alignment_activity": alignment_activity, "existing_strand_flags": existing_strand_flags, "existing_position_flags": existing_position_flags, "asking_vector_map": asking_vector_map, "lookup_address_map": lookup_address_map, "content_vector_map": content_vector_map, "sigmoid_switch_map": sigmoid_switch_map, "final_mixing_map": final_mixing_map, "final_offset_vector": final_offset_vector, "first_factor_map": first_factor_map, "first_factor_offset": first_factor_offset, "second_factor_map": second_factor_map, "second_factor_offset": second_factor_offset, "couple_mixing_map": couple_mixing_map, "couple_change_offset": couple_change_offset}


def standardize_entries(values):
    centered = values - lax.optimization_barrier(jnp.mean(values, axis=-1, keepdims=True))
    spread = lax.optimization_barrier(jnp.mean(centered * centered, axis=-1, keepdims=True))
    return centered * lax.rsqrt(spread + 1e-05)

def reference(alignment_activity, existing_strand_flags, existing_position_flags, asking_vector_map, lookup_address_map, content_vector_map, sigmoid_switch_map, final_mixing_map, final_offset_vector, first_factor_map, first_factor_offset, second_factor_map, second_factor_offset, couple_mixing_map, couple_change_offset):
    standardized_source = standardize_entries(alignment_activity.astype(jnp.float32)).astype(jnp.bfloat16)
    unrolled_tensor = standardized_source.reshape(ALIGNED_STRANDS * CHAIN_LENGTH, ALIGN_DEPTH)
    inv_scale = HEAD_SIZE ** (-0.5)
    queries = (jnp.dot(unrolled_tensor, asking_vector_map, preferred_element_type=jnp.float32) * inv_scale).astype(jnp.bfloat16).reshape(ALIGNED_STRANDS, CHAIN_LENGTH, HEADS, HEAD_SIZE)
    keys_all = jnp.dot(unrolled_tensor, lookup_address_map, preferred_element_type=jnp.float32).astype(jnp.bfloat16).reshape(ALIGNED_STRANDS, CHAIN_LENGTH, HEADS, HEAD_SIZE)
    values_all = jnp.dot(unrolled_tensor, content_vector_map, preferred_element_type=jnp.float32).astype(jnp.bfloat16).reshape(ALIGNED_STRANDS, CHAIN_LENGTH, HEADS, HEAD_SIZE)
    gates = jax.nn.sigmoid(jnp.dot(unrolled_tensor, sigmoid_switch_map, preferred_element_type=jnp.float32)).reshape(ALIGNED_STRANDS, CHAIN_LENGTH, HEADS, HEAD_SIZE)
    keep = existing_strand_flags.astype(jnp.float32)
    key_bias = (keep - 1.0) * 1000000000.0

    def column(residue):
        query_col = lax.dynamic_index_in_dim(queries, residue, 1, keepdims=False).astype(jnp.float32)
        key_col = lax.dynamic_index_in_dim(keys_all, residue, 1, keepdims=False).astype(jnp.float32)
        value_col = lax.dynamic_index_in_dim(values_all, residue, 1, keepdims=False).astype(jnp.float32)
        gate_col = lax.dynamic_index_in_dim(gates, residue, 1, keepdims=False)
        scores = jnp.einsum('shd,thd->hst', query_col, key_col) + key_bias[None, None, :]
        scores = scores - lax.optimization_barrier(jnp.max(scores, axis=-1, keepdims=True))
        weights = jnp.exp(scores)
        weights = (weights / lax.optimization_barrier(jnp.sum(weights, axis=-1, keepdims=True))).astype(jnp.bfloat16)
        mixed = jnp.einsum('hst,thd->shd', weights.astype(jnp.float32), value_col) * gate_col
        return mixed.astype(jnp.bfloat16)
    weighted_mixture = lax.map(column, jnp.arange(CHAIN_LENGTH, dtype=jnp.int32))
    weighted_mixture = jnp.transpose(weighted_mixture, (1, 0, 2, 3)).reshape(ALIGNED_STRANDS * CHAIN_LENGTH, ALIGN_DEPTH)
    vertical_change = (jnp.dot(weighted_mixture, final_mixing_map, preferred_element_type=jnp.float32) + final_offset_vector).astype(jnp.bfloat16).reshape(ALIGNED_STRANDS, CHAIN_LENGTH, ALIGN_DEPTH)
    residue_keep = existing_position_flags.astype(jnp.float32)
    both_masks = keep[:, None, None] * residue_keep[None, :, None]
    left = ((jnp.dot(unrolled_tensor, first_factor_map, preferred_element_type=jnp.float32) + first_factor_offset).reshape(ALIGNED_STRANDS, CHAIN_LENGTH, OUTER_FACTORS) * both_masks).astype(jnp.bfloat16)
    right = ((jnp.dot(unrolled_tensor, second_factor_map, preferred_element_type=jnp.float32) + second_factor_offset).reshape(ALIGNED_STRANDS, CHAIN_LENGTH, OUTER_FACTORS) * both_masks).astype(jnp.bfloat16)
    kept = jnp.sum(keep)
    pair_matrix = couple_mixing_map.reshape(OUTER_FACTORS, OUTER_FACTORS * C_Z)
    right_wide = right.astype(jnp.float32)
    block_size = CHAIN_LENGTH // N_DAP

    def pair_rows(block):
        left_block = lax.dynamic_slice_in_dim(left, block * block_size, block_size, 1)
        projected = jnp.dot(left_block.reshape(ALIGNED_STRANDS * block_size, OUTER_FACTORS), pair_matrix, preferred_element_type=jnp.float32).astype(jnp.bfloat16).reshape(ALIGNED_STRANDS, block_size, OUTER_FACTORS, C_Z)
        return jnp.einsum('sice,sjc->ije', projected.astype(jnp.float32), right_wide)
    total = lax.map(pair_rows, jnp.arange(N_DAP, dtype=jnp.int32)).reshape(CHAIN_LENGTH, CHAIN_LENGTH, C_Z)
    pair_update = (total / kept + couple_change_offset).astype(jnp.bfloat16)
    return (vertical_change, pair_update)
```

```python
import jax
import jax.numpy as jnp
from jax import lax
from jax.experimental import pallas as pl
from jax.experimental.pallas import tpu as pltpu
from jax.sharding import PartitionSpec as P

GROUPS = 16
ROWS = 8
TOKENS = 128
WIDTH = 256
LANES = 128
HEADS = 8
HEAD_SIZE = 32
FACTORS = 32
C_Z = 128
F32 = jnp.float32
BF16 = jnp.bfloat16
MESH = pl.DeviceIdType.MESH


def iota(shape, axis):
    return lax.broadcasted_iota(jnp.int32, shape, axis)


def dot(a, b):
    return jnp.dot(a, b, preferred_element_type=F32)


def pack_halves(wide):
    low = wide[:, :LANES].reshape(GROUPS, ROWS, LANES)
    high = wide[:, LANES:].reshape(GROUPS, ROWS, LANES)
    return jnp.concatenate([low, high], axis=1).astype(BF16)


def unpack_halves(packed):
    tall = packed.astype(F32)
    return (
        tall[:, :ROWS].reshape(TOKENS, LANES),
        tall[:, ROWS:].reshape(TOKENS, LANES),
    )


def swap_blocks(v):
    block = iota(v[0].shape, v[0].ndim - 1) // FACTORS
    odd = block % 2 == 1
    high = block >= 2
    axis = v[0].ndim - 1
    u = [None] * 4
    for a in (0, 2):
        u[a] = jnp.where(odd, pltpu.roll(v[a + 1], 32, axis), v[a])
        u[a + 1] = jnp.where(odd, v[a + 1], pltpu.roll(v[a], 96, axis))
    w = [None] * 4
    for a in (0, 1):
        w[a] = jnp.where(high, pltpu.roll(u[a + 2], 64, axis), u[a])
        w[a + 2] = jnp.where(high, u[a + 2], pltpu.roll(u[a], 64, axis))
    return w


def kernel(
    x_hbm,
    strand_hbm,
    position_hbm,
    wq_hbm,
    wk_hbm,
    wv_hbm,
    wg_hbm,
    wo_hbm,
    bo_hbm,
    w1_hbm,
    b1_hbm,
    w2_hbm,
    b2_hbm,
    wz_hbm,
    bz_hbm,
    column_out,
    pair_out,
    x,
    strand,
    position,
    wq,
    wk,
    wv,
    wg,
    wo,
    bo,
    w1,
    b1,
    w2,
    b2,
    wz,
    bz,
    msa_send,
    msa_recv,
    upd_send,
    upd_recv,
    zbuf,
    lrbuf,
    rbuf,
    total,
    load_sem,
    msa_ssem,
    msa_rsem,
    upd_ssem,
    upd_rsem,
    z_ssem,
    z_rsem,
    lr_ssem,
    lr_rsem,
    r_ssem,
    r_rsem,
):
    d = lax.axis_index("dap")
    q = lax.axis_index("pair")
    z = lax.div(d, 2)
    xl = lax.rem(d, 2)
    other = 1 - xl

    pairs = [
        (x_hbm, x),
        (strand_hbm, strand),
        (position_hbm, position),
        (w1_hbm, w1),
        (b1_hbm, b1),
        (w2_hbm, w2),
        (b2_hbm, b2),
        (wq_hbm, wq),
        (wk_hbm, wk),
        (wv_hbm, wv),
        (wg_hbm, wg),
        (wo_hbm, wo),
        (bo_hbm, bo),
        (wz_hbm, wz),
        (bz_hbm, bz),
    ]
    loads = [pltpu.make_async_copy(a, b, load_sem.at[i]) for i, (a, b) in enumerate(pairs)]
    for load in loads:
        load.start()

    barrier = pltpu.get_barrier_semaphore()

    def greet_line(r, _):
        there = lax.rem(z + r, GROUPS)
        pl.semaphore_signal(barrier, inc=1, device_id=(there * 2 + xl, q), device_id_type=MESH)
        return 0

    def greet_plane(r, _):
        there = lax.rem(xl * GROUPS + q + r, 2 * GROUPS)
        pl.semaphore_signal(
            barrier,
            inc=1,
            device_id=(z * 2 + lax.div(there, GROUPS), lax.rem(there, GROUPS)),
            device_id_type=MESH,
        )
        return 0

    lax.fori_loop(1, GROUPS, greet_line, 0)
    lax.fori_loop(1, 2 * GROUPS, greet_plane, 0)

    loads[0].wait()
    wide = x[...].astype(F32).reshape(TOKENS, WIDTH)
    centered = wide - jnp.mean(wide, axis=-1, keepdims=True)
    spread = jnp.mean(centered * centered, axis=-1, keepdims=True)
    normed = (centered * lax.rsqrt(spread + 1e-05)).astype(BF16)

    row = iota((TOKENS, TOKENS), 0)
    col = iota((TOKENS, TOKENS), 1)
    by_residue = (col == lax.rem(row, ROWS) * GROUPS + lax.div(row, ROWS)).astype(F32).astype(BF16)
    msa_send[...] = pack_halves(dot(by_residue, normed))

    for load in loads[1:7]:
        load.wait()
    keep = strand[...].astype(F32)
    present = position[...].astype(F32)
    keep_rows = jnp.sum(
        jnp.where(col == q * ROWS + lax.div(row, GROUPS), keep, 0.0), axis=-1, keepdims=True
    )
    row4 = iota((TOKENS, 4 * LANES), 0)
    col4 = iota((TOKENS, 4 * LANES), 1)
    residue = lax.rem(row4, GROUPS)
    keep_residues = jnp.sum(
        jnp.where(col4 == d * GROUPS + residue, present, 0.0), axis=-1, keepdims=True
    )
    both = keep_rows * keep_residues
    left = ((dot(normed, w1[...]) + b1[...]) * both).astype(BF16)
    right = ((dot(normed, w2[...]) + b2[...]) * both).astype(BF16)

    factor = iota((FACTORS, 4 * LANES), 0)
    lane = iota((FACTORS, 4 * LANES), 1)
    spread_left = (lax.div(lane, GROUPS) == factor).astype(F32).astype(BF16)
    spread_right = (lax.rem(lane, FACTORS) == factor).astype(F32).astype(BF16)
    pick_row = iota((ROWS, TOKENS), 0)
    pick_col = iota((ROWS, TOKENS), 1)
    pick = (lax.div(pick_col, GROUPS) == pick_row).astype(F32).astype(BF16)
    left_lanes = jnp.where(lax.rem(col4, GROUPS) == residue, dot(left, spread_left), 0.0)
    right_lanes = jnp.where(lax.div(col4, FACTORS) == residue, dot(right, spread_right), 0.0)
    left_rows = dot(pick, left_lanes.astype(BF16))
    right_rows = dot(pick, right_lanes.astype(BF16))

    def fold(rows):
        tiles = [rows[:, LANES * g : LANES * (g + 1)] for g in range(4)]
        return jnp.concatenate(tiles, axis=0).reshape(2, 2 * ROWS, LANES).astype(BF16)

    zbuf[:, 0:2] = jnp.broadcast_to(fold(left_rows)[None], (GROUPS, 2, 2 * ROWS, LANES))
    zbuf[pl.ds(z, 1), 2:4] = fold(right_rows)[None]

    pl.semaphore_wait(barrier, GROUPS - 1 + 2 * GROUPS - 1)

    def send_msa(r, _):
        there = lax.rem(q + r, GROUPS)
        pltpu.make_async_remote_copy(
            src_ref=msa_send.at[there],
            dst_ref=msa_recv.at[q],
            send_sem=msa_ssem,
            recv_sem=msa_rsem,
            device_id=(d, there),
            device_id_type=MESH,
        ).start()
        return 0

    lax.fori_loop(1, GROUPS, send_msa, 0)
    pltpu.make_async_copy(msa_send.at[q], msa_recv.at[q], msa_rsem).start()

    def send_line(r, _):
        there = lax.rem(z + r, GROUPS)
        pltpu.make_async_remote_copy(
            src_ref=zbuf.at[z, pl.ds(2, 2)],
            dst_ref=zbuf.at[z, pl.ds(2, 2)],
            send_sem=z_ssem,
            recv_sem=z_rsem.at[z],
            device_id=(there * 2 + xl, q),
            device_id_type=MESH,
        ).start()
        return 0

    lax.fori_loop(1, GROUPS, send_line, 0)

    def pass_on(r, _):
        there = lax.rem(z + r, GROUPS)

        @pl.when(r > 0)
        def _():
            pltpu.make_async_copy(
                zbuf.at[there, pl.ds(2, 2)], zbuf.at[there, pl.ds(2, 2)], z_rsem.at[there]
            ).wait()

        @pl.when(there != q)
        def _():
            pltpu.make_async_remote_copy(
                src_ref=zbuf.at[there],
                dst_ref=lrbuf.at[q],
                send_sem=lr_ssem,
                recv_sem=lr_rsem,
                device_id=(d, there),
                device_id_type=MESH,
            ).start()

        @pl.when(there == q)
        def _():
            pltpu.make_async_copy(zbuf.at[there], lrbuf.at[q], lr_rsem).start()

        pltpu.make_async_remote_copy(
            src_ref=zbuf.at[there, pl.ds(2, 2)],
            dst_ref=rbuf.at[q],
            send_sem=r_ssem,
            recv_sem=r_rsem,
            device_id=(z * 2 + other, there),
            device_id_type=MESH,
        ).start()
        return 0

    lax.fori_loop(0, 1, pass_on, 0)

    for load in loads[7:11]:
        load.wait()
    pltpu.make_async_copy(msa_recv, msa_recv, msa_rsem).wait()
    items = jnp.concatenate(unpack_halves(msa_recv[...]), axis=1).astype(BF16)
    queries = (dot(items, wq[...]) * HEAD_SIZE ** (-0.5)).astype(BF16)
    keys = dot(items, wk[...]).astype(BF16)
    values = dot(items, wv[...]).astype(BF16)
    gates = jax.nn.sigmoid(dot(items, wg[...]))
    head = lax.div(iota((TOKENS, WIDTH), 1), HEAD_SIZE)
    zero = jnp.zeros((TOKENS, WIDTH), BF16)
    one = jnp.ones((TOKENS, WIDTH), BF16)
    queries_by_head = jnp.concatenate(
        [jnp.where(head == h, queries, zero) for h in range(HEADS)], axis=0
    )
    values_by_head = jnp.concatenate(
        [jnp.where(head == h, values, zero) for h in range(HEADS)], axis=0
    )
    ones_by_head = jnp.concatenate([jnp.where(head == h, one, zero) for h in range(HEADS)], axis=0)
    scores = lax.dot_general(
        queries_by_head, keys, (((1,), (1,)), ((), ())), preferred_element_type=F32
    ) + (keep - 1.0) * 1e9
    weights = jnp.exp(scores - jnp.max(scores, axis=-1, keepdims=True)).astype(BF16)
    weights = jnp.concatenate(
        [weights[h * TOKENS : (h + 1) * TOKENS] for h in range(HEADS)], axis=1
    )
    mixed = dot(weights, values_by_head) / dot(weights, ones_by_head)
    attended = (mixed * gates).astype(BF16)
    loads[11].wait()
    loads[12].wait()
    upd_send[...] = pack_halves(dot(attended, wo[...]) + bo[...])

    def send_update(r, _):
        there = lax.rem(q + r, GROUPS)
        pltpu.make_async_remote_copy(
            src_ref=upd_send.at[there],
            dst_ref=upd_recv.at[q],
            send_sem=upd_ssem,
            recv_sem=upd_rsem,
            device_id=(d, there),
            device_id_type=MESH,
        ).start()
        return 0

    lax.fori_loop(1, GROUPS, send_update, 0)
    pltpu.make_async_copy(upd_send.at[q], upd_recv.at[q], upd_rsem).start()

    lax.fori_loop(1, GROUPS, pass_on, 0)

    pltpu.make_async_copy(upd_recv, upd_recv, upd_rsem).wait()
    by_row = (col == lax.rem(row, GROUPS) * ROWS + lax.div(row, GROUPS)).astype(F32).astype(BF16)
    update = jnp.concatenate(unpack_halves(upd_recv[...]), axis=1).astype(BF16)
    column_out[...] = dot(by_row, update).astype(BF16).reshape(ROWS, GROUPS, WIDTH)

    loads[13].wait()
    loads[14].wait()
    kept = jnp.sum(keep)
    pltpu.make_async_copy(lrbuf, lrbuf, lr_rsem).wait()
    left_t = jnp.concatenate(
        [tile.T for a in range(2) for tile in unpack_halves(lrbuf[:, a])], axis=0
    ).astype(BF16)

    def finish(half, pieces, place):
        rights = jnp.concatenate(
            [tile for piece in pieces for tile in unpack_halves(piece)], axis=1
        ).astype(BF16)
        outer = dot(left_t, rights).reshape(FACTORS, GROUPS, 4 * LANES)
        rows = [[None] * 8 for _ in range(GROUPS)]
        for c in range(8):
            for j in range(4):
                moved = swap_blocks(
                    [outer[4 * c + a, :, LANES * j : LANES * (j + 1)] for a in range(4)]
                )
                for b in range(4):
                    rows[4 * j + b][c] = moved[b].astype(BF16)
        flat = jnp.concatenate([jnp.concatenate(r, axis=1) for r in rows], axis=0)
        sums = dot(flat, wz[...])
        for k in range(GROUPS):
            total[half, pl.ds(k, GROUPS, stride=GROUPS), :] = sums[GROUPS * k : GROUPS * (k + 1)]
        pair_out[:, pl.ds(pl.multiple_of(place * GROUPS, GROUPS), GROUPS), :] = (
            (total[half] / kept + bz[...]).astype(BF16).reshape(GROUPS, GROUPS, C_Z)
        )

    finish(0, [lrbuf[:, 2], lrbuf[:, 3]], xl)
    pltpu.make_async_copy(rbuf, rbuf, r_rsem).wait()
    finish(1, [rbuf[:, 0], rbuf[:, 1]], other)

    some = pl.ds(0, GROUPS - 1)

    def sent(ref, sem):
        pltpu.make_async_copy(ref, ref, sem).wait()

    sent(msa_send.at[some], msa_ssem)
    sent(upd_send.at[some], upd_ssem)
    sent(zbuf.at[some, pl.ds(2, 2)], z_ssem)
    sent(zbuf.at[some], lr_ssem)
    sent(rbuf, r_ssem)


def local(
    alignment_activity,
    existing_strand_flags,
    existing_position_flags,
    asking_vector_map,
    lookup_address_map,
    content_vector_map,
    sigmoid_switch_map,
    final_mixing_map,
    final_offset_vector,
    first_factor_map,
    first_factor_offset,
    second_factor_map,
    second_factor_offset,
    couple_mixing_map,
    couple_change_offset,
):
    args = (
        alignment_activity,
        existing_strand_flags.reshape(1, -1),
        existing_position_flags.reshape(1, -1),
        asking_vector_map,
        lookup_address_map,
        content_vector_map,
        sigmoid_switch_map,
        final_mixing_map,
        final_offset_vector.reshape(1, -1),
        first_factor_map,
        first_factor_offset.reshape(1, -1),
        second_factor_map,
        second_factor_offset.reshape(1, -1),
        couple_mixing_map,
        couple_change_offset.reshape(1, -1),
    )
    piece = (2 * ROWS, LANES)
    return pl.pallas_call(
        kernel,
        out_shape=(
            jax.ShapeDtypeStruct((ROWS, GROUPS, WIDTH), BF16),
            jax.ShapeDtypeStruct((GROUPS, 2 * GROUPS, C_Z), BF16),
        ),
        in_specs=[pl.BlockSpec(memory_space=pl.ANY)] * len(args),
        out_specs=[pl.BlockSpec(memory_space=pltpu.VMEM)] * 2,
        scratch_shapes=[pltpu.VMEM(a.shape, a.dtype) for a in args]
        + [
            pltpu.VMEM((GROUPS, *piece), BF16),
            pltpu.VMEM((GROUPS, *piece), BF16),
            pltpu.VMEM((GROUPS, *piece), BF16),
            pltpu.VMEM((GROUPS, *piece), BF16),
            pltpu.VMEM((GROUPS, 4, *piece), BF16),
            pltpu.VMEM((GROUPS, 4, *piece), BF16),
            pltpu.VMEM((GROUPS, 2, *piece), BF16),
            pltpu.VMEM((2, WIDTH, C_Z), F32),
            pltpu.SemaphoreType.DMA((len(args),)),
            pltpu.SemaphoreType.DMA,
            pltpu.SemaphoreType.DMA,
            pltpu.SemaphoreType.DMA,
            pltpu.SemaphoreType.DMA,
            pltpu.SemaphoreType.DMA,
            pltpu.SemaphoreType.DMA((GROUPS,)),
            pltpu.SemaphoreType.DMA,
            pltpu.SemaphoreType.DMA,
            pltpu.SemaphoreType.DMA,
            pltpu.SemaphoreType.DMA,
        ],
        compiler_params=pltpu.CompilerParams(
            collective_id=0, has_side_effects=True, vmem_limit_bytes=32 * 1024 * 1024
        ),
        name="column_attention_and_outer_mean",
    )(*args)


def solution(mesh):
    return jax.shard_map(
        local,
        mesh=mesh,
        in_specs=(P("pair", "dap", None),) + (P(),) * 14,
        out_specs=(P("pair", "dap", None), P("dap", "pair", None)),
        check_vma=False,
    )
```

```python
import jax
import jax.numpy as jnp
from jax import lax
from jax.experimental import pallas as pl
from jax.experimental.pallas import tpu as pltpu
from jax.sharding import PartitionSpec as P

GROUPS = 16
ROWS = 8
TOKENS = 128
WIDTH = 256
LANES = 128
HEADS = 8
HEAD_SIZE = 32
FACTORS = 32
C_Z = 128
EARLY = 8
F32 = jnp.float32
BF16 = jnp.bfloat16
MESH = pl.DeviceIdType.MESH


def iota(shape, axis):
    return lax.broadcasted_iota(jnp.int32, shape, axis)


def dot(a, b):
    return jnp.dot(a, b, preferred_element_type=F32)


def dot_t(a, b):
    return lax.dot_general(a, b, (((1,), (1,)), ((), ())), preferred_element_type=F32)


def pack_halves(wide):
    low = wide[:, :LANES].reshape(GROUPS, ROWS, LANES)
    high = wide[:, LANES:].reshape(GROUPS, ROWS, LANES)
    return jnp.concatenate([low, high], axis=1).astype(BF16)


def unpack_halves(packed):
    tall = packed.astype(F32)
    return (
        tall[:, :ROWS].reshape(TOKENS, LANES),
        tall[:, ROWS:].reshape(TOKENS, LANES),
    )


def swap_blocks(v):
    block = iota(v[0].shape, v[0].ndim - 1) // FACTORS
    odd = block % 2 == 1
    high = block >= 2
    axis = v[0].ndim - 1
    u = [None] * 4
    for a in (0, 2):
        u[a] = jnp.where(odd, pltpu.roll(v[a + 1], 32, axis), v[a])
        u[a + 1] = jnp.where(odd, v[a + 1], pltpu.roll(v[a], 96, axis))
    w = [None] * 4
    for a in (0, 1):
        w[a] = jnp.where(high, pltpu.roll(u[a + 2], 64, axis), u[a])
        w[a + 2] = jnp.where(high, u[a + 2], pltpu.roll(u[a], 64, axis))
    return w


def kernel(
    x_hbm,
    strand_hbm,
    position_hbm,
    wq_hbm,
    wk_hbm,
    wv_hbm,
    wg_hbm,
    wo_hbm,
    bo_hbm,
    w1_hbm,
    b1_hbm,
    w2_hbm,
    b2_hbm,
    wz_hbm,
    bz_hbm,
    column_out,
    pair_out,
    x,
    strand,
    position,
    wq,
    wk,
    wv,
    wg,
    wo,
    bo,
    w1,
    b1,
    w2,
    b2,
    wz,
    bz,
    msa_send,
    msa_recv,
    upd_send,
    upd_recv,
    zbuf,
    rbuf,
    total,
    load_sem,
    msa_ssem,
    msa_rsem,
    upd_ssem,
    upd_rsem,
    z_ssem,
    z_rsem,
    r_ssem,
    r_rsem,
    ready,
):
    d = lax.axis_index("dap")
    q = lax.axis_index("pair")
    z = lax.div(d, 2)
    xl = lax.rem(d, 2)
    other = 1 - xl

    pairs = [
        (x_hbm, x),
        (strand_hbm, strand),
        (position_hbm, position),
        (w1_hbm, w1),
        (b1_hbm, b1),
        (w2_hbm, w2),
        (b2_hbm, b2),
        (wq_hbm, wq),
        (wk_hbm, wk),
        (wv_hbm, wv),
        (wg_hbm, wg),
        (wo_hbm, wo),
        (bo_hbm, bo),
        (wz_hbm, wz),
        (bz_hbm, bz),
    ]
    loads = [pltpu.make_async_copy(a, b, load_sem.at[i]) for i, (a, b) in enumerate(pairs)]
    for load in loads:
        load.start()

    barrier = pltpu.get_barrier_semaphore()

    def line(there):
        return (there * 2 + xl, q)

    def greet_line(there, _):
        pl.semaphore_signal(barrier, inc=1, device_id=line(there), device_id_type=MESH)
        return 0

    def greet_plane(r, _):
        there = lax.rem(xl * GROUPS + q + r, 2 * GROUPS)
        pl.semaphore_signal(
            barrier,
            inc=1,
            device_id=(z * 2 + lax.div(there, GROUPS), lax.rem(there, GROUPS)),
            device_id_type=MESH,
        )
        return 0

    lax.fori_loop(1, 2 * GROUPS, greet_plane, 0)
    lax.fori_loop(z + 1, GROUPS, greet_line, 0)

    loads[0].wait()
    wide = x[...].astype(F32).reshape(TOKENS, WIDTH)
    centered = wide - jnp.mean(wide, axis=-1, keepdims=True)
    spread = jnp.mean(centered * centered, axis=-1, keepdims=True)
    normed = (centered * lax.rsqrt(spread + 1e-05)).astype(BF16)

    row = iota((TOKENS, TOKENS), 0)
    col = iota((TOKENS, TOKENS), 1)
    by_residue = (col == lax.rem(row, ROWS) * GROUPS + lax.div(row, ROWS)).astype(F32).astype(BF16)
    for load in loads[1:7]:
        load.wait()
    keep = strand[...].astype(F32)
    present = position[...].astype(F32)
    keep_rows = jnp.sum(
        jnp.where(col == q * ROWS + lax.div(row, GROUPS), keep, 0.0), axis=-1, keepdims=True
    )
    row4 = iota((TOKENS, 4 * LANES), 0)
    col4 = iota((TOKENS, 4 * LANES), 1)
    residue = lax.rem(row4, GROUPS)
    keep_residues = jnp.sum(
        jnp.where(col4 == d * GROUPS + residue, present, 0.0), axis=-1, keepdims=True
    )
    both = keep_rows * keep_residues
    left = ((dot_t(normed, w1[...]) + b1[...]) * both).astype(BF16)
    right = ((dot_t(normed, w2[...]) + b2[...]) * both).astype(BF16)

    factor = iota((FACTORS, 4 * LANES), 0)
    lane = iota((FACTORS, 4 * LANES), 1)
    spread_left = (lax.div(lane, GROUPS) == factor).astype(F32).astype(BF16)
    spread_right = (lax.rem(lane, FACTORS) == factor).astype(F32).astype(BF16)
    pick_row = iota((ROWS, TOKENS), 0)
    pick_col = iota((ROWS, TOKENS), 1)
    pick = (lax.div(pick_col, GROUPS) == pick_row).astype(F32).astype(BF16)
    left_lanes = jnp.where(lax.rem(col4, GROUPS) == residue, dot(left, spread_left), 0.0)
    right_lanes = jnp.where(lax.div(col4, FACTORS) == residue, dot(right, spread_right), 0.0)
    right_rows = dot(pick, right_lanes.astype(BF16))

    def fold(rows):
        tiles = [rows[:, LANES * g : LANES * (g + 1)] for g in range(4)]
        return jnp.concatenate(tiles, axis=0).reshape(1, 2, 2 * ROWS, LANES).astype(BF16)

    zbuf[pl.ds(z, 1)] = fold(right_rows)
    msa_send[:, 0] = pack_halves(dot(by_residue, normed))
    left_rows = dot(pick, left_lanes.astype(BF16))
    msa_send[:, 1:3] = jnp.broadcast_to(fold(left_rows), (GROUPS, 2, 2 * ROWS, LANES))

    pl.semaphore_wait(barrier, 2 * GROUPS - 1 + z)

    def send_line(there, _):
        pltpu.make_async_remote_copy(
            src_ref=zbuf.at[z],
            dst_ref=zbuf.at[z],
            send_sem=z_ssem,
            recv_sem=z_rsem.at[z],
            device_id=line(there),
            device_id_type=MESH,
        ).start()
        return 0

    def answer_line(there, _):
        pl.semaphore_signal(ready.at[z], inc=1, device_id=line(there), device_id_type=MESH)
        return 0

    def send_when_ready(there, _):
        pl.semaphore_wait(ready.at[there], 1)
        return send_line(there, 0)

    lax.fori_loop(0, z, send_line, 0)
    lax.fori_loop(0, z, answer_line, 0)

    def send_msa(r, _):
        there = lax.rem(q + r, GROUPS)
        pltpu.make_async_remote_copy(
            src_ref=msa_send.at[there],
            dst_ref=msa_recv.at[q],
            send_sem=msa_ssem,
            recv_sem=msa_rsem,
            device_id=(d, there),
            device_id_type=MESH,
        ).start()
        return 0

    lax.fori_loop(1, GROUPS, send_msa, 0)
    pltpu.make_async_copy(msa_send.at[q], msa_recv.at[q], msa_rsem).start()

    def pass_on(there):
        @pl.when(there != q)
        def _():
            pltpu.make_async_remote_copy(
                src_ref=zbuf.at[there],
                dst_ref=rbuf.at[xl, q],
                send_sem=r_ssem,
                recv_sem=r_rsem.at[xl],
                device_id=(d, there),
                device_id_type=MESH,
            ).start()

        @pl.when(there == q)
        def _():
            pltpu.make_async_copy(zbuf.at[there], rbuf.at[xl, q], r_rsem.at[xl]).start()

        pltpu.make_async_remote_copy(
            src_ref=zbuf.at[there],
            dst_ref=rbuf.at[xl, q],
            send_sem=r_ssem,
            recv_sem=r_rsem.at[xl],
            device_id=(z * 2 + other, there),
            device_id_type=MESH,
        ).start()

    pass_on(z)

    early = z < EARLY

    def exchange(i, _):
        there = jnp.where(early, jnp.where(i < EARLY, i, 23 - i), lax.rem(i + EARLY, GROUPS))

        @pl.when(jnp.logical_and(early, there >= EARLY))
        def _():
            send_when_ready(there, 0)

        @pl.when(there != z)
        def _():
            pltpu.make_async_copy(zbuf.at[there], zbuf.at[there], z_rsem.at[there]).wait()
            pass_on(there)

        return 0

    for load in loads[7:11]:
        load.wait()
    pltpu.make_async_copy(msa_recv, msa_recv, msa_rsem).wait()
    items = jnp.concatenate(unpack_halves(msa_recv[:, 0]), axis=1).astype(BF16)
    queries = (dot(items, wq[...]) * HEAD_SIZE ** (-0.5)).astype(BF16)
    keys = dot(items, wk[...]).astype(BF16)
    values = dot(items, wv[...]).astype(BF16)
    gates = jax.nn.sigmoid(dot(items, wg[...]))
    head = lax.div(iota((TOKENS, WIDTH), 1), HEAD_SIZE)
    zero = jnp.zeros((TOKENS, WIDTH), BF16)
    one = jnp.ones((TOKENS, WIDTH), BF16)
    queries_by_head = jnp.concatenate(
        [jnp.where(head == h, queries, zero) for h in range(HEADS)], axis=0
    )
    values_by_head = jnp.concatenate(
        [jnp.where(head == h, values, zero) for h in range(HEADS)], axis=0
    )
    ones_by_head = jnp.concatenate([jnp.where(head == h, one, zero) for h in range(HEADS)], axis=0)
    scores = dot_t(queries_by_head, keys) + (keep - 1.0) * 1e9
    weights = jnp.exp(scores - jnp.max(scores, axis=-1, keepdims=True)).astype(BF16)
    weights = jnp.concatenate(
        [weights[h * TOKENS : (h + 1) * TOKENS] for h in range(HEADS)], axis=1
    )
    mixed = dot(weights, values_by_head) / dot(weights, ones_by_head)
    attended = (mixed * gates).astype(BF16)
    loads[11].wait()
    loads[12].wait()
    upd_send[...] = pack_halves(dot(attended, wo[...]) + bo[...])

    def send_update(r, _):
        there = lax.rem(q + r, GROUPS)
        pltpu.make_async_remote_copy(
            src_ref=upd_send.at[there],
            dst_ref=upd_recv.at[q],
            send_sem=upd_ssem,
            recv_sem=upd_rsem,
            device_id=(d, there),
            device_id_type=MESH,
        ).start()
        return 0

    lax.fori_loop(1, GROUPS, send_update, 0)
    pltpu.make_async_copy(upd_send.at[q], upd_recv.at[q], upd_rsem).start()

    lax.fori_loop(z + 1, jnp.where(early, EARLY, GROUPS), send_when_ready, 0)
    lax.fori_loop(0, EARLY, exchange, 0)

    pltpu.make_async_copy(upd_recv, upd_recv, upd_rsem).wait()
    by_row = (col == lax.rem(row, GROUPS) * ROWS + lax.div(row, GROUPS)).astype(F32).astype(BF16)
    update = jnp.concatenate(unpack_halves(upd_recv[...]), axis=1).astype(BF16)
    column_out[...] = dot(by_row, update).astype(BF16).reshape(ROWS, GROUPS, WIDTH)

    left_t = jnp.concatenate(
        [tile.T for a in (1, 2) for tile in unpack_halves(msa_recv[:, a])], axis=0
    ).astype(BF16)
    loads[13].wait()
    loads[14].wait()
    kept = jnp.sum(keep)

    lax.fori_loop(EARLY, GROUPS, exchange, 0)

    for half in range(2):
        pltpu.make_async_copy(rbuf.at[half], rbuf.at[half], r_rsem.at[half]).wait()
        rights = jnp.concatenate(
            [tile for a in range(2) for tile in unpack_halves(rbuf[half, :, a])], axis=1
        ).astype(BF16)
        outer = dot(left_t, rights).reshape(FACTORS, GROUPS, 4 * LANES)
        rows = [[None] * 8 for _ in range(GROUPS)]
        for c in range(8):
            for j in range(4):
                moved = swap_blocks(
                    [outer[4 * c + a, :, LANES * j : LANES * (j + 1)] for a in range(4)]
                )
                for b in range(4):
                    rows[4 * j + b][c] = moved[b].astype(BF16)
        flat = jnp.concatenate([jnp.concatenate(r, axis=1) for r in rows], axis=0)
        sums = dot(flat, wz[...])
        for k in range(GROUPS):
            total[half, pl.ds(k, GROUPS, stride=GROUPS), :] = sums[GROUPS * k : GROUPS * (k + 1)]
        pair_out[:, half * GROUPS : (half + 1) * GROUPS, :] = (
            (total[half] / kept + bz[...]).astype(BF16).reshape(GROUPS, GROUPS, C_Z)
        )

    some = pl.ds(0, GROUPS - 1)

    def sent(ref, sem):
        pltpu.make_async_copy(ref, ref, sem).wait()

    sent(msa_send.at[some], msa_ssem)
    sent(upd_send.at[some], upd_ssem)
    sent(zbuf.at[some], z_ssem)
    sent(zbuf, r_ssem)
    sent(zbuf.at[some], r_ssem)


def local(
    alignment_activity,
    existing_strand_flags,
    existing_position_flags,
    asking_vector_map,
    lookup_address_map,
    content_vector_map,
    sigmoid_switch_map,
    final_mixing_map,
    final_offset_vector,
    first_factor_map,
    first_factor_offset,
    second_factor_map,
    second_factor_offset,
    couple_mixing_map,
    couple_change_offset,
):
    args = (
        alignment_activity,
        existing_strand_flags.reshape(1, -1),
        existing_position_flags.reshape(1, -1),
        asking_vector_map,
        lookup_address_map,
        content_vector_map,
        sigmoid_switch_map,
        final_mixing_map,
        final_offset_vector.reshape(1, -1),
        first_factor_map.T,
        first_factor_offset.reshape(1, -1),
        second_factor_map.T,
        second_factor_offset.reshape(1, -1),
        couple_mixing_map,
        couple_change_offset.reshape(1, -1),
    )
    piece = (2 * ROWS, LANES)
    return pl.pallas_call(
        kernel,
        out_shape=(
            jax.ShapeDtypeStruct((ROWS, GROUPS, WIDTH), BF16),
            jax.ShapeDtypeStruct((GROUPS, 2 * GROUPS, C_Z), BF16),
        ),
        in_specs=[pl.BlockSpec(memory_space=pl.ANY)] * len(args),
        out_specs=[pl.BlockSpec(memory_space=pltpu.VMEM)] * 2,
        scratch_shapes=[pltpu.VMEM(a.shape, a.dtype) for a in args]
        + [
            pltpu.VMEM((GROUPS, 3, *piece), BF16),
            pltpu.VMEM((GROUPS, 3, *piece), BF16),
            pltpu.VMEM((GROUPS, *piece), BF16),
            pltpu.VMEM((GROUPS, *piece), BF16),
            pltpu.VMEM((GROUPS, 2, *piece), BF16),
            pltpu.VMEM((2, GROUPS, 2, *piece), BF16),
            pltpu.VMEM((2, WIDTH, C_Z), F32),
            pltpu.SemaphoreType.DMA((len(args),)),
            pltpu.SemaphoreType.DMA,
            pltpu.SemaphoreType.DMA,
            pltpu.SemaphoreType.DMA,
            pltpu.SemaphoreType.DMA,
            pltpu.SemaphoreType.DMA,
            pltpu.SemaphoreType.DMA((GROUPS,)),
            pltpu.SemaphoreType.DMA,
            pltpu.SemaphoreType.DMA((2,)),
            pltpu.SemaphoreType.REGULAR((GROUPS,)),
        ],
        compiler_params=pltpu.CompilerParams(
            collective_id=0, has_side_effects=True, vmem_limit_bytes=60 * 1024 * 1024
        ),
        name="column_attention_and_outer_mean",
    )(*args)


def solution(mesh):
    return jax.shard_map(
        local,
        mesh=mesh,
        in_specs=(P("pair", "dap", None),) + (P(),) * 14,
        out_specs=(P("pair", "dap", None), P("dap", "pair", None)),
        check_vma=False,
    )
```

```python
import jax
import jax.numpy as jnp
from jax import lax
from jax.experimental import pallas as pl
from jax.experimental.pallas import tpu as pltpu
from jax.sharding import PartitionSpec as P

GROUPS = 16
ROWS = 8
TOKENS = 128
WIDTH = 256
LANES = 128
HEADS = 8
HEAD_SIZE = 32
FACTORS = 32
C_Z = 128
EARLY = 8
NEAR = 4
F32 = jnp.float32
BF16 = jnp.bfloat16
MESH = pl.DeviceIdType.MESH


def iota(shape, axis):
    return lax.broadcasted_iota(jnp.int32, shape, axis)


def dot(a, b):
    return jnp.dot(a, b, preferred_element_type=F32)


def dot_t(a, b):
    return lax.dot_general(a, b, (((1,), (1,)), ((), ())), preferred_element_type=F32)


def pack_halves(wide):
    low = wide[:, :LANES].reshape(GROUPS, ROWS, LANES)
    high = wide[:, LANES:].reshape(GROUPS, ROWS, LANES)
    return jnp.concatenate([low, high], axis=1).astype(BF16)


def unpack_halves(packed):
    tall = packed.astype(F32)
    return (
        tall[:, :ROWS].reshape(TOKENS, LANES),
        tall[:, ROWS:].reshape(TOKENS, LANES),
    )


def swap_blocks(v):
    block = iota(v[0].shape, v[0].ndim - 1) // FACTORS
    odd = block % 2 == 1
    high = block >= 2
    axis = v[0].ndim - 1
    u = [None] * 4
    for a in (0, 2):
        u[a] = jnp.where(odd, pltpu.roll(v[a + 1], 32, axis), v[a])
        u[a + 1] = jnp.where(odd, v[a + 1], pltpu.roll(v[a], 96, axis))
    w = [None] * 4
    for a in (0, 1):
        w[a] = jnp.where(high, pltpu.roll(u[a + 2], 64, axis), u[a])
        w[a + 2] = jnp.where(high, u[a + 2], pltpu.roll(u[a], 64, axis))
    return w


def kernel(
    x_hbm,
    strand_hbm,
    position_hbm,
    wq_hbm,
    wk_hbm,
    wv_hbm,
    wg_hbm,
    wo_hbm,
    bo_hbm,
    w1_hbm,
    b1_hbm,
    w2_hbm,
    b2_hbm,
    wz_hbm,
    bz_hbm,
    column_out,
    pair_out,
    x,
    strand,
    position,
    wq,
    wk,
    wv,
    wg,
    wo,
    bo,
    w1,
    b1,
    w2,
    b2,
    wz,
    bz,
    msa_send,
    msa_recv,
    upd_send,
    upd_recv,
    lbuf,
    zbuf,
    rbuf,
    total,
    load_sem,
    msa_ssem,
    msa_rsem,
    upd_ssem,
    upd_rsem,
    l_ssem,
    l_rsem,
    z_ssem,
    z_rsem,
    r_ssem,
    r_rsem,
    ready,
):
    d = lax.axis_index("dap")
    q = lax.axis_index("pair")
    z = lax.div(d, 2)
    xl = lax.rem(d, 2)
    other = 1 - xl

    y, xh, core = lax.div(q, 4), lax.rem(lax.div(q, 2), 2), lax.rem(q, 2)
    steps = [(2, 1), (1, 1), (3, 1), (2, 0), (0, 1), (1, 0), (3, 0), (0, 0)]
    partners = [
        lax.rem(y + a, 4) * 4 + lax.rem(xh + b, 2) * 2 + lax.rem(core + e, 2)
        for a, b in steps
        for e in (0, 1)
        if a + b + e > 0
    ]

    pairs = [
        (x_hbm, x),
        (strand_hbm, strand),
        (position_hbm, position),
        (w1_hbm, w1),
        (b1_hbm, b1),
        (w2_hbm, w2),
        (b2_hbm, b2),
        (wq_hbm, wq),
        (wk_hbm, wk),
        (wv_hbm, wv),
        (wg_hbm, wg),
        (wo_hbm, wo),
        (bo_hbm, bo),
        (wz_hbm, wz),
        (bz_hbm, bz),
    ]
    loads = [pltpu.make_async_copy(a, b, load_sem.at[i]) for i, (a, b) in enumerate(pairs)]
    for load in loads:
        load.start()

    barrier = pltpu.get_barrier_semaphore()

    def line(there):
        return (there * 2 + xl, q)

    def greet_line(there, _):
        pl.semaphore_signal(barrier, inc=1, device_id=line(there), device_id_type=MESH)
        return 0

    def greet_plane(r, _):
        there = lax.rem(xl * GROUPS + q + r, 2 * GROUPS)
        pl.semaphore_signal(
            barrier,
            inc=1,
            device_id=(z * 2 + lax.div(there, GROUPS), lax.rem(there, GROUPS)),
            device_id_type=MESH,
        )
        return 0

    lax.fori_loop(1, 2 * GROUPS, greet_plane, 0)
    lax.fori_loop(z + 1, GROUPS, greet_line, 0)

    loads[0].wait()
    wide = x[...].astype(F32).reshape(TOKENS, WIDTH)
    centered = wide - jnp.mean(wide, axis=-1, keepdims=True)
    spread = jnp.mean(centered * centered, axis=-1, keepdims=True)
    normed = (centered * lax.rsqrt(spread + 1e-05)).astype(BF16)

    row = iota((TOKENS, TOKENS), 0)
    col = iota((TOKENS, TOKENS), 1)
    by_residue = (col == lax.rem(row, ROWS) * GROUPS + lax.div(row, ROWS)).astype(F32).astype(BF16)
    for load in loads[1:7]:
        load.wait()
    keep = strand[...].astype(F32)
    present = position[...].astype(F32)
    keep_rows = jnp.sum(
        jnp.where(col == q * ROWS + lax.div(row, GROUPS), keep, 0.0), axis=-1, keepdims=True
    )
    row4 = iota((TOKENS, 4 * LANES), 0)
    col4 = iota((TOKENS, 4 * LANES), 1)
    residue = lax.rem(row4, GROUPS)
    keep_residues = jnp.sum(
        jnp.where(col4 == d * GROUPS + residue, present, 0.0), axis=-1, keepdims=True
    )
    both = keep_rows * keep_residues
    left = ((dot_t(normed, w1[...]) + b1[...]) * both).astype(BF16)
    right = ((dot_t(normed, w2[...]) + b2[...]) * both).astype(BF16)

    factor = iota((FACTORS, 4 * LANES), 0)
    lane = iota((FACTORS, 4 * LANES), 1)
    spread_left = (lax.div(lane, GROUPS) == factor).astype(F32).astype(BF16)
    spread_right = (lax.rem(lane, FACTORS) == factor).astype(F32).astype(BF16)
    pick_row = iota((ROWS, TOKENS), 0)
    pick_col = iota((ROWS, TOKENS), 1)
    pick = (lax.div(pick_col, GROUPS) == pick_row).astype(F32).astype(BF16)
    left_lanes = jnp.where(lax.rem(col4, GROUPS) == residue, dot(left, spread_left), 0.0)
    right_lanes = jnp.where(lax.div(col4, FACTORS) == residue, dot(right, spread_right), 0.0)
    right_rows = dot(pick, right_lanes.astype(BF16))

    def fold(rows):
        tiles = [rows[:, LANES * g : LANES * (g + 1)] for g in range(4)]
        return jnp.concatenate(tiles, axis=0).reshape(1, 2, 2 * ROWS, LANES).astype(BF16)

    zbuf[pl.ds(z, 1)] = fold(right_rows)
    msa_send[...] = pack_halves(dot(by_residue, normed))
    left_rows = dot(pick, left_lanes.astype(BF16))
    lbuf[pl.ds(q, 1)] = fold(left_rows)

    pl.semaphore_wait(barrier, 2 * GROUPS - 1 + z)

    def send_line(there, _):
        pltpu.make_async_remote_copy(
            src_ref=zbuf.at[z],
            dst_ref=zbuf.at[z],
            send_sem=z_ssem,
            recv_sem=z_rsem.at[z],
            device_id=line(there),
            device_id_type=MESH,
        ).start()
        return 0

    def answer_line(there, _):
        pl.semaphore_signal(ready.at[z], inc=1, device_id=line(there), device_id_type=MESH)
        return 0

    def send_when_ready(there, _):
        pl.semaphore_wait(ready.at[there], 1)
        return send_line(there, 0)

    lax.fori_loop(0, z, send_line, 0)
    lax.fori_loop(0, z, answer_line, 0)

    def send_rows(out, into, send_sem, recv_sem):
        for there in partners:
            pltpu.make_async_remote_copy(
                src_ref=out.at[there],
                dst_ref=into.at[q],
                send_sem=send_sem,
                recv_sem=recv_sem,
                device_id=(d, there),
                device_id_type=MESH,
            ).start()
        pltpu.make_async_copy(out.at[q], into.at[q], recv_sem).start()

    send_rows(msa_send, msa_recv, msa_ssem, msa_rsem)

    def pass_on(there):
        @pl.when(there != q)
        def _():
            pltpu.make_async_remote_copy(
                src_ref=zbuf.at[there],
                dst_ref=rbuf.at[xl, q],
                send_sem=r_ssem,
                recv_sem=r_rsem.at[xl],
                device_id=(d, there),
                device_id_type=MESH,
            ).start()

        @pl.when(there == q)
        def _():
            pltpu.make_async_copy(zbuf.at[there], rbuf.at[xl, q], r_rsem.at[xl]).start()

        pltpu.make_async_remote_copy(
            src_ref=zbuf.at[there],
            dst_ref=rbuf.at[xl, q],
            send_sem=r_ssem,
            recv_sem=r_rsem.at[xl],
            device_id=(z * 2 + other, there),
            device_id_type=MESH,
        ).start()

    pass_on(z)
    for there in partners:
        pltpu.make_async_remote_copy(
            src_ref=lbuf.at[q],
            dst_ref=lbuf.at[q],
            send_sem=l_ssem,
            recv_sem=l_rsem,
            device_id=(d, there),
            device_id_type=MESH,
        ).start()

    some = pl.ds(0, GROUPS - 1)

    def sent(ref, sem):
        pltpu.make_async_copy(ref, ref, sem).wait()

    def take(there):
        pltpu.make_async_copy(zbuf.at[there], zbuf.at[there], z_rsem.at[there]).wait()
        pass_on(there)

    early = z < EARLY
    first = jnp.where(early, 0, EARLY)
    last = first + EARLY

    def near_send(step, _):
        @pl.when(z + step < last)
        def _():
            send_when_ready(z + step, 0)

        return 0

    def near_take(step, _):
        @pl.when(z + step < last)
        def _():
            take(z + step)

        @pl.when(z - step >= first)
        def _():
            take(z - step)

        return 0

    def across(i):
        return jnp.where(
            early,
            jnp.where(z < EARLY // 2, GROUPS - 1 - i, EARLY + i),
            jnp.where(z < EARLY + EARLY // 2, EARLY - 1 - i, i),
        )

    def across_send(i, _):
        return send_when_ready(across(i), 0)

    def across_take(i, _):
        take(across(i))
        return 0

    lax.fori_loop(1, NEAR, near_send, 0)
    lax.fori_loop(1, NEAR, near_take, 0)

    for load in loads[7:11]:
        load.wait()
    pltpu.make_async_copy(msa_recv, msa_recv, msa_rsem).wait()
    items = jnp.concatenate(unpack_halves(msa_recv[...]), axis=1).astype(BF16)
    queries = (dot(items, wq[...]) * HEAD_SIZE ** (-0.5)).astype(BF16)
    keys = dot(items, wk[...]).astype(BF16)
    values = dot(items, wv[...]).astype(BF16)
    gates = jax.nn.sigmoid(dot(items, wg[...]))
    head = lax.div(iota((TOKENS, WIDTH), 1), HEAD_SIZE)
    zero = jnp.zeros((TOKENS, WIDTH), BF16)
    one = jnp.ones((TOKENS, WIDTH), BF16)
    queries_by_head = jnp.concatenate(
        [jnp.where(head == h, queries, zero) for h in range(HEADS)], axis=0
    )
    values_by_head = jnp.concatenate(
        [jnp.where(head == h, values, zero) for h in range(HEADS)], axis=0
    )
    ones_by_head = jnp.concatenate([jnp.where(head == h, one, zero) for h in range(HEADS)], axis=0)
    scores = dot_t(queries_by_head, keys) + (keep - 1.0) * 1e9
    weights = jnp.exp(scores - jnp.max(scores, axis=-1, keepdims=True)).astype(BF16)
    weights = jnp.concatenate(
        [weights[h * TOKENS : (h + 1) * TOKENS] for h in range(HEADS)], axis=1
    )
    mixed = dot(weights, values_by_head) / dot(weights, ones_by_head)
    attended = (mixed * gates).astype(BF16)
    loads[11].wait()
    loads[12].wait()
    upd_send[...] = pack_halves(dot(attended, wo[...]) + bo[...])

    send_rows(upd_send, upd_recv, upd_ssem, upd_rsem)

    lax.fori_loop(NEAR, EARLY, near_send, 0)
    lax.fori_loop(0, jnp.where(jnp.logical_and(early, z >= EARLY // 2), EARLY, 0), across_send, 0)
    lax.fori_loop(NEAR, EARLY, near_take, 0)
    lax.fori_loop(0, jnp.where(z < EARLY // 2, EARLY, 0), across_send, 0)
    lax.fori_loop(0, EARLY, across_take, 0)

    pltpu.make_async_copy(upd_recv, upd_recv, upd_rsem).wait()
    by_row = (col == lax.rem(row, GROUPS) * ROWS + lax.div(row, GROUPS)).astype(F32).astype(BF16)
    update = jnp.concatenate(unpack_halves(upd_recv[...]), axis=1).astype(BF16)
    column_out[...] = dot(by_row, update).astype(BF16).reshape(ROWS, GROUPS, WIDTH)

    sent(lbuf.at[some], l_rsem)
    left_t = jnp.concatenate(
        [tile.T for a in range(2) for tile in unpack_halves(lbuf[:, a])], axis=0
    ).astype(BF16)
    loads[13].wait()
    loads[14].wait()
    kept = jnp.sum(keep)

    for half in range(2):
        pltpu.make_async_copy(rbuf.at[half], rbuf.at[half], r_rsem.at[half]).wait()
        rights = jnp.concatenate(
            [tile for a in range(2) for tile in unpack_halves(rbuf[half, :, a])], axis=1
        ).astype(BF16)
        outer = dot(left_t, rights).reshape(FACTORS, GROUPS, 4 * LANES)
        rows = [[None] * 8 for _ in range(GROUPS)]
        for c in range(8):
            for j in range(4):
                moved = swap_blocks(
                    [outer[4 * c + a, :, LANES * j : LANES * (j + 1)] for a in range(4)]
                )
                for b in range(4):
                    rows[4 * j + b][c] = moved[b].astype(BF16)
        flat = jnp.concatenate([jnp.concatenate(r, axis=1) for r in rows], axis=0)
        sums = dot(flat, wz[...])
        for k in range(GROUPS):
            total[half, pl.ds(k, GROUPS, stride=GROUPS), :] = sums[GROUPS * k : GROUPS * (k + 1)]
        pair_out[:, half * GROUPS : (half + 1) * GROUPS, :] = (
            (total[half] / kept + bz[...]).astype(BF16).reshape(GROUPS, GROUPS, C_Z)
        )

    sent(lbuf.at[some], l_ssem)
    sent(msa_send.at[some], msa_ssem)
    sent(upd_send.at[some], upd_ssem)
    sent(zbuf.at[some], z_ssem)
    sent(zbuf, r_ssem)
    sent(zbuf.at[some], r_ssem)


def local(
    alignment_activity,
    existing_strand_flags,
    existing_position_flags,
    asking_vector_map,
    lookup_address_map,
    content_vector_map,
    sigmoid_switch_map,
    final_mixing_map,
    final_offset_vector,
    first_factor_map,
    first_factor_offset,
    second_factor_map,
    second_factor_offset,
    couple_mixing_map,
    couple_change_offset,
):
    args = (
        alignment_activity,
        existing_strand_flags.reshape(1, -1),
        existing_position_flags.reshape(1, -1),
        asking_vector_map,
        lookup_address_map,
        content_vector_map,
        sigmoid_switch_map,
        final_mixing_map,
        final_offset_vector.reshape(1, -1),
        first_factor_map.T,
        first_factor_offset.reshape(1, -1),
        second_factor_map.T,
        second_factor_offset.reshape(1, -1),
        couple_mixing_map,
        couple_change_offset.reshape(1, -1),
    )
    piece = (2 * ROWS, LANES)
    return pl.pallas_call(
        kernel,
        out_shape=(
            jax.ShapeDtypeStruct((ROWS, GROUPS, WIDTH), BF16),
            jax.ShapeDtypeStruct((GROUPS, 2 * GROUPS, C_Z), BF16),
        ),
        in_specs=[pl.BlockSpec(memory_space=pl.ANY)] * len(args),
        out_specs=[pl.BlockSpec(memory_space=pltpu.VMEM)] * 2,
        scratch_shapes=[pltpu.VMEM(a.shape, a.dtype) for a in args]
        + [
            pltpu.VMEM((GROUPS, *piece), BF16),
            pltpu.VMEM((GROUPS, *piece), BF16),
            pltpu.VMEM((GROUPS, *piece), BF16),
            pltpu.VMEM((GROUPS, *piece), BF16),
            pltpu.VMEM((GROUPS, 2, *piece), BF16),
            pltpu.VMEM((GROUPS, 2, *piece), BF16),
            pltpu.VMEM((2, GROUPS, 2, *piece), BF16),
            pltpu.VMEM((2, WIDTH, C_Z), F32),
            pltpu.SemaphoreType.DMA((len(args),)),
            pltpu.SemaphoreType.DMA,
            pltpu.SemaphoreType.DMA,
            pltpu.SemaphoreType.DMA,
            pltpu.SemaphoreType.DMA,
            pltpu.SemaphoreType.DMA,
            pltpu.SemaphoreType.DMA,
            pltpu.SemaphoreType.DMA,
            pltpu.SemaphoreType.DMA((GROUPS,)),
            pltpu.SemaphoreType.DMA,
            pltpu.SemaphoreType.DMA((2,)),
            pltpu.SemaphoreType.REGULAR((GROUPS,)),
        ],
        compiler_params=pltpu.CompilerParams(
            collective_id=0, has_side_effects=True, vmem_limit_bytes=16 * 1024 * 1024
        ),
        name="column_attention_and_outer_mean",
    )(*[pltpu.with_memory_space_constraint(a, pltpu.HBM) for a in args])


def solution(mesh):
    return jax.shard_map(
        local,
        mesh=mesh,
        in_specs=(P("pair", "dap", None),) + (P(),) * 14,
        out_specs=(P("pair", "dap", None), P("dap", "pair", None)),
        check_vma=False,
    )
```

```python
import jax
import jax.numpy as jnp
from jax import lax
from jax.experimental import pallas as pl
from jax.experimental.pallas import tpu as pltpu
from jax.sharding import PartitionSpec as P

GROUPS = 16
ROWS = 8
TOKENS = 128
WIDTH = 256
LANES = 128
HEADS = 8
HEAD_SIZE = 32
FACTORS = 32
C_Z = 128
BLOCK = 8
REACH = 4
F32 = jnp.float32
BF16 = jnp.bfloat16
MESH = pl.DeviceIdType.MESH


def iota(shape, axis):
    return lax.broadcasted_iota(jnp.int32, shape, axis)


def dot(a, b):
    return jnp.dot(a, b, preferred_element_type=F32)


def dot_t(a, b):
    return lax.dot_general(a, b, (((1,), (1,)), ((), ())), preferred_element_type=F32)


def pack_halves(wide):
    low = wide[:, :LANES].reshape(GROUPS, ROWS, LANES)
    high = wide[:, LANES:].reshape(GROUPS, ROWS, LANES)
    return jnp.concatenate([low, high], axis=1).astype(BF16)


def unpack_halves(packed):
    tall = packed.astype(F32)
    return (
        tall[:, :ROWS].reshape(TOKENS, LANES),
        tall[:, ROWS:].reshape(TOKENS, LANES),
    )


def swap_blocks(v):
    block = iota(v[0].shape, v[0].ndim - 1) // FACTORS
    odd = block % 2 == 1
    high = block >= 2
    axis = v[0].ndim - 1
    u = [None] * 4
    for a in (0, 2):
        u[a] = jnp.where(odd, pltpu.roll(v[a + 1], 32, axis), v[a])
        u[a + 1] = jnp.where(odd, v[a + 1], pltpu.roll(v[a], 96, axis))
    w = [None] * 4
    for a in (0, 1):
        w[a] = jnp.where(high, pltpu.roll(u[a + 2], 64, axis), u[a])
        w[a + 2] = jnp.where(high, u[a + 2], pltpu.roll(u[a], 64, axis))
    return w


def kernel(
    x_hbm,
    strand_hbm,
    position_hbm,
    wq_hbm,
    wk_hbm,
    wv_hbm,
    wg_hbm,
    wo_hbm,
    bo_hbm,
    w1_hbm,
    b1_hbm,
    w2_hbm,
    b2_hbm,
    wz_hbm,
    bz_hbm,
    column_out,
    pair_out,
    x,
    strand,
    position,
    wq,
    wk,
    wv,
    wg,
    wo,
    bo,
    w1,
    b1,
    w2,
    b2,
    wz,
    bz,
    msa_send,
    msa_recv,
    upd_send,
    upd_recv,
    lbuf,
    zbuf,
    rbuf,
    total,
    load_sem,
    msa_ssem,
    msa_rsem,
    upd_ssem,
    upd_rsem,
    l_ssem,
    l_rsem,
    across_ssem,
    near_ssem,
    relay_ssem,
    z_rsem,
    r_ssem,
    r_rsem,
    ready,
):
    d = lax.axis_index("dap")
    q = lax.axis_index("pair")
    z = lax.div(d, 2)
    xl = lax.rem(d, 2)
    other = 1 - xl

    pairs = [
        (x_hbm, x),
        (strand_hbm, strand),
        (position_hbm, position),
        (w1_hbm, w1),
        (b1_hbm, b1),
        (w2_hbm, w2),
        (b2_hbm, b2),
        (wq_hbm, wq),
        (wk_hbm, wk),
        (wv_hbm, wv),
        (wg_hbm, wg),
        (wo_hbm, wo),
        (bo_hbm, bo),
        (wz_hbm, wz),
        (bz_hbm, bz),
    ]
    loads = [pltpu.make_async_copy(a, b, load_sem.at[i]) for i, (a, b) in enumerate(pairs)]
    loads[0].start()

    y, xh, core = lax.div(q, 4), lax.rem(lax.div(q, 2), 2), lax.rem(q, 2)
    steps = [(2, 1), (1, 1), (3, 1), (2, 0), (0, 1), (1, 0), (3, 0), (0, 0)]
    partners = [
        lax.rem(y + a, 4) * 4 + lax.rem(xh + b, 2) * 2 + lax.rem(core + e, 2)
        for a, b in steps
        for e in (0, 1)
        if a + b + e > 0
    ]

    barrier = pltpu.get_barrier_semaphore()

    def line(there):
        return (there * 2 + xl, q)

    early = z < BLOCK
    first = jnp.where(early, 0, BLOCK)
    last = first + BLOCK
    reach = jnp.where(early, BLOCK, REACH)
    reach_low = jnp.maximum(z - reach, first)
    reach_high = jnp.minimum(z + reach + 1, last)
    before = jnp.where(early, REACH - 1, REACH)
    before_high = jnp.minimum(z + before + 1, last)
    below = jnp.where(early, 0, BLOCK)

    def greet_line(there, _):
        pl.semaphore_signal(barrier, inc=1, device_id=line(there), device_id_type=MESH)
        return 0

    def greet(there_d, there_q):
        pl.semaphore_signal(barrier, inc=1, device_id=(there_d, there_q), device_id_type=MESH)

    lax.fori_loop(z + 1, reach_high, greet_line, 0)
    lax.fori_loop(BLOCK, BLOCK + BLOCK - below, greet_line, 0)
    for there in partners:
        greet(z * 2 + other, there)
        greet(d, there)
    greet(z * 2 + other, q)

    for load in loads[1:]:
        load.start()

    loads[0].wait()
    wide = x[...].astype(F32).reshape(TOKENS, WIDTH)
    centered = wide - jnp.mean(wide, axis=-1, keepdims=True)
    spread = jnp.mean(centered * centered, axis=-1, keepdims=True)
    normed = (centered * lax.rsqrt(spread + 1e-05)).astype(BF16)

    row = iota((TOKENS, TOKENS), 0)
    col = iota((TOKENS, TOKENS), 1)
    by_residue = (col == lax.rem(row, ROWS) * GROUPS + lax.div(row, ROWS)).astype(F32).astype(BF16)
    for load in loads[1:7]:
        load.wait()
    keep = strand[...].astype(F32)
    present = position[...].astype(F32)
    keep_rows = jnp.sum(
        jnp.where(col == q * ROWS + lax.div(row, GROUPS), keep, 0.0), axis=-1, keepdims=True
    )
    row4 = iota((TOKENS, 4 * LANES), 0)
    col4 = iota((TOKENS, 4 * LANES), 1)
    residue = lax.rem(row4, GROUPS)
    keep_residues = jnp.sum(
        jnp.where(col4 == d * GROUPS + residue, present, 0.0), axis=-1, keepdims=True
    )
    both = keep_rows * keep_residues
    left = ((dot_t(normed, w1[...]) + b1[...]) * both).astype(BF16)
    right = ((dot_t(normed, w2[...]) + b2[...]) * both).astype(BF16)

    factor = iota((FACTORS, 4 * LANES), 0)
    lane = iota((FACTORS, 4 * LANES), 1)
    spread_left = (lax.div(lane, GROUPS) == factor).astype(F32).astype(BF16)
    spread_right = (lax.rem(lane, FACTORS) == factor).astype(F32).astype(BF16)
    pick_row = iota((ROWS, TOKENS), 0)
    pick_col = iota((ROWS, TOKENS), 1)
    pick = (lax.div(pick_col, GROUPS) == pick_row).astype(F32).astype(BF16)
    left_lanes = jnp.where(lax.rem(col4, GROUPS) == residue, dot(left, spread_left), 0.0)
    right_lanes = jnp.where(lax.div(col4, FACTORS) == residue, dot(right, spread_right), 0.0)
    right_rows = dot(pick, right_lanes.astype(BF16))

    def fold(rows):
        tiles = [rows[:, LANES * g : LANES * (g + 1)] for g in range(4)]
        return jnp.concatenate(tiles, axis=0).reshape(1, 2, 2 * ROWS, LANES).astype(BF16)

    zbuf[pl.ds(z, 1)] = fold(right_rows)
    msa_send[...] = pack_halves(dot(by_residue, normed))
    left_rows = dot(pick, left_lanes.astype(BF16))
    lbuf[pl.ds(q, 1)] = fold(left_rows)

    pl.semaphore_wait(barrier, 2 * GROUPS - 1 + z - reach_low + below)

    def send_piece(piece, there, sem):
        pltpu.make_async_remote_copy(
            src_ref=zbuf.at[piece],
            dst_ref=zbuf.at[piece],
            send_sem=sem,
            recv_sem=z_rsem.at[piece],
            device_id=line(there),
            device_id_type=MESH,
        ).start()

    def send_across(there, _):
        send_piece(z, there, across_ssem)
        return 0

    def send_near(there, _):
        send_piece(z, there, near_ssem.at[there])
        return 0

    def answer_line(there, _):
        pl.semaphore_signal(ready.at[z], inc=1, device_id=line(there), device_id_type=MESH)
        return 0

    lax.fori_loop(0, below, send_across, 0)
    lax.fori_loop(reach_low, z, send_near, 0)
    lax.fori_loop(0, below, answer_line, 0)
    lax.fori_loop(reach_low, z, answer_line, 0)

    def send_rows(out, into, send_sem, recv_sem):
        for there in partners:
            pltpu.make_async_remote_copy(
                src_ref=out.at[there],
                dst_ref=into.at[q],
                send_sem=send_sem,
                recv_sem=recv_sem,
                device_id=(d, there),
                device_id_type=MESH,
            ).start()
        pltpu.make_async_copy(out.at[q], into.at[q], recv_sem).start()

    send_rows(msa_send, msa_recv, msa_ssem, msa_rsem)

    def pass_on(there):
        @pl.when(there != q)
        def _():
            pltpu.make_async_remote_copy(
                src_ref=zbuf.at[there],
                dst_ref=rbuf.at[xl, q],
                send_sem=r_ssem,
                recv_sem=r_rsem.at[xl],
                device_id=(d, there),
                device_id_type=MESH,
            ).start()

        @pl.when(there == q)
        def _():
            pltpu.make_async_copy(zbuf.at[there], rbuf.at[xl, q], r_rsem.at[xl]).start()

        pltpu.make_async_remote_copy(
            src_ref=zbuf.at[there],
            dst_ref=rbuf.at[xl, q],
            send_sem=r_ssem,
            recv_sem=r_rsem.at[xl],
            device_id=(z * 2 + other, there),
            device_id_type=MESH,
        ).start()

    pass_on(z)

    some = pl.ds(0, GROUPS - 1)

    def sent(ref, sem):
        pltpu.make_async_copy(ref, ref, sem).wait()

    def take(there):
        pltpu.make_async_copy(zbuf.at[there], zbuf.at[there], z_rsem.at[there]).wait()
        pass_on(there)

    def near_send(there, _):
        pl.semaphore_wait(ready.at[there], 1)
        return send_near(there, 0)

    def near_take(step, _):
        @pl.when(z + step < last)
        def _():
            take(z + step)

        @pl.when(z - step >= first)
        def _():
            take(z - step)

        return 0

    def relay(away):
        piece = z + away

        @pl.when(jnp.logical_and(jnp.logical_not(early), jnp.logical_and(piece >= first, piece < last)))
        def _():
            take(piece)
            for i in range(1, REACH):
                there = z - i if away > 0 else z + i

                @pl.when(jnp.logical_and(there >= first, there < last))
                def _():
                    send_piece(piece, there, relay_ssem.at[i])

    def across(i):
        return jnp.where(
            early,
            jnp.where(z < BLOCK // 2, GROUPS - 1 - i, BLOCK + i),
            jnp.where(z < BLOCK + BLOCK // 2, BLOCK - 1 - i, i),
        )

    def across_send(i, _):
        there = across(i)
        pl.semaphore_wait(ready.at[there], 1)
        return send_across(there, 0)

    def across_take(i, _):
        take(across(i))
        return 0

    lax.fori_loop(z + 1, before_high, near_send, 0)
    lax.fori_loop(1, REACH, near_take, 0)

    for load in loads[7:11]:
        load.wait()
    pltpu.make_async_copy(msa_recv, msa_recv, msa_rsem).wait()
    items = jnp.concatenate(unpack_halves(msa_recv[...]), axis=1).astype(BF16)
    queries = (dot(items, wq[...]) * HEAD_SIZE ** (-0.5)).astype(BF16)
    keys = dot(items, wk[...]).astype(BF16)
    values = dot(items, wv[...]).astype(BF16)
    gates = jax.nn.sigmoid(dot(items, wg[...]))
    head = lax.div(iota((TOKENS, WIDTH), 1), HEAD_SIZE)
    zero = jnp.zeros((TOKENS, WIDTH), BF16)
    one = jnp.ones((TOKENS, WIDTH), BF16)
    queries_by_head = jnp.concatenate(
        [jnp.where(head == h, queries, zero) for h in range(HEADS)], axis=0
    )
    values_by_head = jnp.concatenate(
        [jnp.where(head == h, values, zero) for h in range(HEADS)], axis=0
    )
    ones_by_head = jnp.concatenate([jnp.where(head == h, one, zero) for h in range(HEADS)], axis=0)
    scores = dot_t(queries_by_head, keys) + (keep - 1.0) * 1e9
    weights = jnp.exp(scores - jnp.max(scores, axis=-1, keepdims=True)).astype(BF16)
    weights = jnp.concatenate(
        [weights[h * TOKENS : (h + 1) * TOKENS] for h in range(HEADS)], axis=1
    )
    mixed = dot(weights, values_by_head) / dot(weights, ones_by_head)
    attended = (mixed * gates).astype(BF16)
    loads[11].wait()
    loads[12].wait()
    upd_send[...] = pack_halves(dot(attended, wo[...]) + bo[...])

    send_rows(upd_send, upd_recv, upd_ssem, upd_rsem)
    for there in partners:
        pltpu.make_async_remote_copy(
            src_ref=lbuf.at[q],
            dst_ref=lbuf.at[q],
            send_sem=l_ssem,
            recv_sem=l_rsem,
            device_id=(d, there),
            device_id_type=MESH,
        ).start()

    relay(REACH)
    relay(-REACH)
    lax.fori_loop(before_high, reach_high, near_send, 0)
    lax.fori_loop(0, jnp.where(jnp.logical_and(early, z >= BLOCK // 2), BLOCK, 0), across_send, 0)
    lax.fori_loop(before + 1, BLOCK, near_take, 0)
    lax.fori_loop(0, jnp.where(z < BLOCK // 2, BLOCK, 0), across_send, 0)
    lax.fori_loop(0, BLOCK, across_take, 0)

    pltpu.make_async_copy(upd_recv, upd_recv, upd_rsem).wait()
    by_row = (col == lax.rem(row, GROUPS) * ROWS + lax.div(row, GROUPS)).astype(F32).astype(BF16)
    update = jnp.concatenate(unpack_halves(upd_recv[...]), axis=1).astype(BF16)
    column_out[...] = dot(by_row, update).astype(BF16).reshape(ROWS, GROUPS, WIDTH)

    sent(lbuf.at[some], l_rsem)
    left_t = jnp.concatenate(
        [tile.T for a in range(2) for tile in unpack_halves(lbuf[:, a])], axis=0
    ).astype(BF16)
    loads[13].wait()
    loads[14].wait()
    kept = jnp.sum(keep)

    for half in range(2):
        pltpu.make_async_copy(rbuf.at[half], rbuf.at[half], r_rsem.at[half]).wait()
        rights = jnp.concatenate(
            [tile for a in range(2) for tile in unpack_halves(rbuf[half, :, a])], axis=1
        ).astype(BF16)
        outer = dot(left_t, rights).astype(BF16).reshape(FACTORS, GROUPS, 4 * LANES)
        rows = [[None] * 8 for _ in range(GROUPS)]
        for c in range(8):
            for j in range(4):
                moved = swap_blocks(
                    [outer[4 * c + a, :, LANES * j : LANES * (j + 1)] for a in range(4)]
                )
                for b in range(4):
                    rows[4 * j + b][c] = moved[b]
        flat = jnp.concatenate([jnp.concatenate(r, axis=1) for r in rows], axis=0)
        sums = dot(flat, wz[...])
        for k in range(GROUPS):
            total[half, pl.ds(k, GROUPS, stride=GROUPS), :] = sums[GROUPS * k : GROUPS * (k + 1)]
        pair_out[:, half * GROUPS : (half + 1) * GROUPS, :] = (
            (total[half] / kept + bz[...]).astype(BF16).reshape(GROUPS, GROUPS, C_Z)
        )

    sent(lbuf.at[some], l_ssem)
    sent(msa_send.at[some], msa_ssem)
    sent(upd_send.at[some], upd_ssem)
    sent(zbuf.at[pl.ds(0, BLOCK)], across_ssem)

    def near_sent(there, _):
        @pl.when(there != z)
        def _():
            sent(zbuf.at[0], near_ssem.at[there])

        return 0

    lax.fori_loop(reach_low, reach_high, near_sent, 0)
    for i in range(1, REACH):
        up = jnp.logical_and(z - REACH >= first, z + i < last)
        down = jnp.logical_and(z + REACH < last, z - i >= first)

        @pl.when(jnp.logical_and(jnp.logical_not(early), jnp.logical_or(up, down)))
        def _():
            sent(zbuf.at[0], relay_ssem.at[i])

    sent(zbuf, r_ssem)
    sent(zbuf.at[some], r_ssem)


def store(column, pair, column_out, pair_out, sem):
    copies = [
        pltpu.make_async_copy(pair, pair_out, sem.at[0]),
        pltpu.make_async_copy(column, column_out, sem.at[1]),
    ]
    for copy in copies:
        copy.start()
    for copy in copies:
        copy.wait()


def local(
    alignment_activity,
    existing_strand_flags,
    existing_position_flags,
    asking_vector_map,
    lookup_address_map,
    content_vector_map,
    sigmoid_switch_map,
    final_mixing_map,
    final_offset_vector,
    first_factor_map,
    first_factor_offset,
    second_factor_map,
    second_factor_offset,
    couple_mixing_map,
    couple_change_offset,
):
    args = (
        alignment_activity,
        existing_strand_flags.reshape(1, -1),
        existing_position_flags.reshape(1, -1),
        asking_vector_map,
        lookup_address_map,
        content_vector_map,
        sigmoid_switch_map,
        final_mixing_map,
        final_offset_vector.reshape(1, -1),
        first_factor_map.T,
        first_factor_offset.reshape(1, -1),
        second_factor_map.T,
        second_factor_offset.reshape(1, -1),
        couple_mixing_map,
        couple_change_offset.reshape(1, -1),
    )
    piece = (2 * ROWS, LANES)
    results = pl.pallas_call(
        kernel,
        out_shape=(
            jax.ShapeDtypeStruct((ROWS, GROUPS, WIDTH), BF16),
            jax.ShapeDtypeStruct((GROUPS, 2 * GROUPS, C_Z), BF16),
        ),
        in_specs=[pl.BlockSpec(memory_space=pl.ANY)] * len(args),
        out_specs=[pl.BlockSpec(memory_space=pltpu.VMEM)] * 2,
        scratch_shapes=[pltpu.VMEM(a.shape, a.dtype) for a in args]
        + [
            pltpu.VMEM((GROUPS, *piece), BF16),
            pltpu.VMEM((GROUPS, *piece), BF16),
            pltpu.VMEM((GROUPS, *piece), BF16),
            pltpu.VMEM((GROUPS, *piece), BF16),
            pltpu.VMEM((GROUPS, 2, *piece), BF16),
            pltpu.VMEM((GROUPS, 2, *piece), BF16),
            pltpu.VMEM((2, GROUPS, 2, *piece), BF16),
            pltpu.VMEM((2, WIDTH, C_Z), F32),
            pltpu.SemaphoreType.DMA((len(args),)),
            pltpu.SemaphoreType.DMA,
            pltpu.SemaphoreType.DMA,
            pltpu.SemaphoreType.DMA,
            pltpu.SemaphoreType.DMA,
            pltpu.SemaphoreType.DMA,
            pltpu.SemaphoreType.DMA,
            pltpu.SemaphoreType.DMA,
            pltpu.SemaphoreType.DMA((GROUPS,)),
            pltpu.SemaphoreType.DMA((REACH,)),
            pltpu.SemaphoreType.DMA((GROUPS,)),
            pltpu.SemaphoreType.DMA,
            pltpu.SemaphoreType.DMA((2,)),
            pltpu.SemaphoreType.REGULAR((GROUPS,)),
        ],
        compiler_params=pltpu.CompilerParams(
            collective_id=0, has_side_effects=True, vmem_limit_bytes=16 * 1024 * 1024
        ),
        name="column_attention_and_outer_mean",
    )(*[pltpu.with_memory_space_constraint(a, pltpu.HBM) for a in args])
    return pl.pallas_call(
        store,
        out_shape=tuple(jax.ShapeDtypeStruct(r.shape, r.dtype) for r in results),
        in_specs=[pl.BlockSpec(memory_space=pltpu.VMEM)] * 2,
        out_specs=[pl.BlockSpec(memory_space=pltpu.HBM)] * 2,
        scratch_shapes=[pltpu.SemaphoreType.DMA((2,))],
        compiler_params=pltpu.CompilerParams(vmem_limit_bytes=2 * 1024 * 1024),
        name="store_results",
    )(*[pltpu.with_memory_space_constraint(r, pltpu.VMEM) for r in results])


def solution(mesh):
    return jax.shard_map(
        local,
        mesh=mesh,
        in_specs=(P("pair", "dap", None),) + (P(),) * 14,
        out_specs=(P("pair", "dap", None), P("dap", "pair", None)),
        check_vma=False,
    )
```

```python
import jax
import jax.numpy as jnp
from jax import lax
from jax.experimental import pallas as pl
from jax.experimental.pallas import tpu as pltpu
from jax.sharding import PartitionSpec as P

GROUPS = 16
ROWS = 8
TOKENS = 128
WIDTH = 256
LANES = 128
HEADS = 8
HEAD_SIZE = 32
FACTORS = 32
C_Z = 128
BLOCK = 8
QUAD = 4
REACH = 4
F32 = jnp.float32
BF16 = jnp.bfloat16
MESH = pl.DeviceIdType.MESH


def iota(shape, axis):
    return lax.broadcasted_iota(jnp.int32, shape, axis)


def dot(a, b):
    return jnp.dot(a, b, preferred_element_type=F32)


def dot_t(a, b):
    return lax.dot_general(a, b, (((1,), (1,)), ((), ())), preferred_element_type=F32)


def pack_halves(wide):
    low = wide[:, :LANES].reshape(GROUPS, ROWS, LANES)
    high = wide[:, LANES:].reshape(GROUPS, ROWS, LANES)
    return jnp.concatenate([low, high], axis=1).astype(BF16)


def unpack_halves(packed):
    tall = packed.astype(F32)
    return (
        tall[:, :ROWS].reshape(TOKENS, LANES),
        tall[:, ROWS:].reshape(TOKENS, LANES),
    )


def kernel(
    x_hbm,
    strand_hbm,
    position_hbm,
    wq_hbm,
    wk_hbm,
    wv_hbm,
    wg_hbm,
    wo_hbm,
    bo_hbm,
    w1_hbm,
    b1_hbm,
    w2_hbm,
    b2_hbm,
    wz_hbm,
    bz_hbm,
    column_out,
    pair_out,
    x,
    strand,
    position,
    wq,
    wk,
    wv,
    wg,
    wo,
    bo,
    w1,
    b1,
    w2,
    b2,
    wz,
    bz,
    msa_send,
    msa_recv,
    upd_send,
    upd_recv,
    lbuf,
    zbuf,
    rbuf,
    total,
    load_sem,
    msa_ssem,
    msa_rsem,
    upd_ssem,
    upd_rsem,
    l_ssem,
    l_rsem,
    across_ssem,
    far_ssem,
    near_ssem,
    relay_ssem,
    z_rsem,
    r_ssem,
    r_rsem,
    ready,
):
    d = lax.axis_index("dap")
    q = lax.axis_index("pair")
    z = lax.div(d, 2)
    xl = lax.rem(d, 2)
    other = 1 - xl

    pairs = [
        (x_hbm, x),
        (strand_hbm, strand),
        (position_hbm, position),
        (w1_hbm, w1),
        (b1_hbm, b1),
        (w2_hbm, w2),
        (b2_hbm, b2),
        (wq_hbm, wq),
        (wk_hbm, wk),
        (wv_hbm, wv),
        (wg_hbm, wg),
        (wo_hbm, wo),
        (bo_hbm, bo),
        (wz_hbm, wz),
        (bz_hbm, bz),
    ]
    loads = [pltpu.make_async_copy(a, b, load_sem.at[i]) for i, (a, b) in enumerate(pairs)]
    loads[0].start()

    y, xh, core = lax.div(q, 4), lax.rem(lax.div(q, 2), 2), lax.rem(q, 2)
    steps = [(2, 1), (1, 1), (3, 1), (2, 0), (0, 1), (1, 0), (3, 0), (0, 0)]
    partners = [
        lax.rem(y + a, 4) * 4 + lax.rem(xh + b, 2) * 2 + lax.rem(core + e, 2)
        for a, b in steps
        for e in (0, 1)
        if a + b + e > 0
    ]

    barrier = pltpu.get_barrier_semaphore()

    def line(there):
        return (there * 2 + xl, q)

    quad = lax.div(z, QUAD)
    early = z < BLOCK
    first = jnp.where(early, 0, BLOCK)
    last = first + BLOCK
    reach = jnp.where(early, BLOCK, REACH)
    reach_low = jnp.maximum(z - reach, first)
    reach_high = jnp.minimum(z + reach + 1, last)
    before = jnp.where(early, REACH - 1, REACH)
    before_high = jnp.minimum(z + before + 1, last)
    below = jnp.where(early, 0, BLOCK)

    def greet_line(there, _):
        pl.semaphore_signal(barrier, inc=1, device_id=line(there), device_id_type=MESH)
        return 0

    def greet(there_d, there_q):
        pl.semaphore_signal(barrier, inc=1, device_id=(there_d, there_q), device_id_type=MESH)

    lax.fori_loop(z + 1, reach_high, greet_line, 0)
    lax.fori_loop(BLOCK, BLOCK + BLOCK - below, greet_line, 0)
    for there in partners:
        greet(z * 2 + other, there)
        greet(d, there)
    greet(z * 2 + other, q)

    for load in loads[1:]:
        load.start()

    loads[0].wait()
    wide = x[...].astype(F32).reshape(TOKENS, WIDTH)
    centered = wide - jnp.mean(wide, axis=-1, keepdims=True)
    spread = jnp.mean(centered * centered, axis=-1, keepdims=True)
    normed = (centered * lax.rsqrt(spread + 1e-05)).astype(BF16)

    row = iota((TOKENS, TOKENS), 0)
    col = iota((TOKENS, TOKENS), 1)
    by_residue = (col == lax.rem(row, ROWS) * GROUPS + lax.div(row, ROWS)).astype(F32).astype(BF16)
    for load in loads[1:7]:
        load.wait()
    keep = strand[...].astype(F32)
    present = position[...].astype(F32)
    keep_rows = jnp.sum(
        jnp.where(col == q * ROWS + lax.div(row, GROUPS), keep, 0.0), axis=-1, keepdims=True
    )
    row4 = iota((TOKENS, 4 * LANES), 0)
    col4 = iota((TOKENS, 4 * LANES), 1)
    residue = lax.rem(row4, GROUPS)
    keep_residues = jnp.sum(
        jnp.where(col4 == d * GROUPS + residue, present, 0.0), axis=-1, keepdims=True
    )
    both = keep_rows * keep_residues
    left = ((dot_t(normed, w1[...]) + b1[...]) * both).astype(BF16)
    right = ((dot_t(normed, w2[...]) + b2[...]) * both).astype(BF16)

    factor = iota((FACTORS, 4 * LANES), 0)
    lane = iota((FACTORS, 4 * LANES), 1)
    spread_left = (lax.div(lane, GROUPS) == factor).astype(F32).astype(BF16)
    spread_right = (lax.rem(lane, FACTORS) == factor).astype(F32).astype(BF16)
    pick_row = iota((ROWS, TOKENS), 0)
    pick_col = iota((ROWS, TOKENS), 1)
    pick = (lax.div(pick_col, GROUPS) == pick_row).astype(F32).astype(BF16)
    left_lanes = jnp.where(lax.rem(col4, GROUPS) == residue, dot(left, spread_left), 0.0)
    right_lanes = jnp.where(lax.div(col4, FACTORS) == residue, dot(right, spread_right), 0.0)
    right_rows = dot(pick, right_lanes.astype(BF16))

    def fold(rows):
        tiles = [rows[:, LANES * g : LANES * (g + 1)] for g in range(4)]
        return jnp.concatenate(tiles, axis=0).reshape(1, 2, 2 * ROWS, LANES).astype(BF16)

    zbuf[pl.ds(z, 1)] = fold(right_rows)
    msa_send[...] = pack_halves(dot(by_residue, normed))
    left_rows = dot(pick, left_lanes.astype(BF16))
    lbuf[pl.ds(q, 1)] = fold(left_rows)

    pl.semaphore_wait(barrier, 2 * GROUPS - 1 + z - reach_low + below)

    def send_piece(piece, there, sem):
        pltpu.make_async_remote_copy(
            src_ref=zbuf.at[piece],
            dst_ref=zbuf.at[piece],
            send_sem=sem,
            recv_sem=z_rsem.at[piece],
            device_id=line(there),
            device_id_type=MESH,
        ).start()

    def send_across(there, _):
        send_piece(z, there, across_ssem)
        return 0

    def send_near(there, _):
        send_piece(z, there, near_ssem.at[there])
        return 0

    def answer_line(there, _):
        pl.semaphore_signal(ready.at[z], inc=1, device_id=line(there), device_id_type=MESH)
        return 0

    lax.fori_loop(0, jnp.where(quad == 3, QUAD, below), send_across, 0)
    lax.fori_loop(reach_low, z, send_near, 0)
    lax.fori_loop(0, below, answer_line, 0)
    lax.fori_loop(reach_low, z, answer_line, 0)

    def send_rows(out, into, send_sem, recv_sem):
        for there in partners:
            pltpu.make_async_remote_copy(
                src_ref=out.at[there],
                dst_ref=into.at[q],
                send_sem=send_sem,
                recv_sem=recv_sem,
                device_id=(d, there),
                device_id_type=MESH,
            ).start()
        pltpu.make_async_copy(out.at[q], into.at[q], recv_sem).start()

    send_rows(msa_send, msa_recv, msa_ssem, msa_rsem)

    def pass_on(there):
        @pl.when(there != q)
        def _():
            pltpu.make_async_remote_copy(
                src_ref=zbuf.at[there],
                dst_ref=rbuf.at[xl, q],
                send_sem=r_ssem,
                recv_sem=r_rsem.at[xl],
                device_id=(d, there),
                device_id_type=MESH,
            ).start()

        @pl.when(there == q)
        def _():
            pltpu.make_async_copy(zbuf.at[there], rbuf.at[xl, q], r_rsem.at[xl]).start()

        pltpu.make_async_remote_copy(
            src_ref=zbuf.at[there],
            dst_ref=rbuf.at[xl, q],
            send_sem=r_ssem,
            recv_sem=r_rsem.at[xl],
            device_id=(z * 2 + other, there),
            device_id_type=MESH,
        ).start()

    pass_on(z)

    some = pl.ds(0, GROUPS - 1)

    def sent(ref, sem):
        pltpu.make_async_copy(ref, ref, sem).wait()

    def take(there):
        pltpu.make_async_copy(zbuf.at[there], zbuf.at[there], z_rsem.at[there]).wait()
        pass_on(there)

    def near_send(there, _):
        pl.semaphore_wait(ready.at[there], 1)
        return send_near(there, 0)

    def near_take(step, _):
        @pl.when(z + step < last)
        def _():
            take(z + step)

        @pl.when(z - step >= first)
        def _():
            take(z - step)

        return 0

    def relay(away):
        piece = z + away

        @pl.when(jnp.logical_and(jnp.logical_not(early), jnp.logical_and(piece >= first, piece < last)))
        def _():
            take(piece)
            for i in range(1, REACH):
                there = z - i if away > 0 else z + i

                @pl.when(jnp.logical_and(there >= first, there < last))
                def _():
                    send_piece(piece, there, relay_ssem.at[i])

    def across_send(i, _):
        there = jnp.where(quad == 0, GROUPS - 1 - i, BLOCK + i)
        pl.semaphore_wait(ready.at[there], 1)
        return send_across(there, 0)

    def across_take(i, _):
        here = i < QUAD
        piece = jnp.where(
            early,
            jnp.where(
                quad == 0,
                jnp.where(jnp.logical_or(here, z < 2), GROUPS - 1 - i, QUAD + i),
                BLOCK + i,
            ),
            jnp.where(quad == 2, BLOCK - 1 - i, i),
        )
        take(piece)

        @pl.when(jnp.logical_and(here, quad == 0))
        def _():
            send_piece(piece, z + QUAD, far_ssem)

        return 0

    lax.fori_loop(z + 1, before_high, near_send, 0)
    for there in partners:
        pltpu.make_async_remote_copy(
            src_ref=lbuf.at[q],
            dst_ref=lbuf.at[q],
            send_sem=l_ssem,
            recv_sem=l_rsem,
            device_id=(d, there),
            device_id_type=MESH,
        ).start()
    lax.fori_loop(1, REACH, near_take, 0)

    for load in loads[7:11]:
        load.wait()
    pltpu.make_async_copy(msa_recv, msa_recv, msa_rsem).wait()
    items = jnp.concatenate(unpack_halves(msa_recv[...]), axis=1).astype(BF16)
    queries = (dot(items, wq[...]) * HEAD_SIZE ** (-0.5)).astype(BF16)
    keys = dot(items, wk[...]).astype(BF16)
    values = dot(items, wv[...]).astype(BF16)
    gates = jax.nn.sigmoid(dot(items, wg[...]))
    head = lax.div(iota((TOKENS, WIDTH), 1), HEAD_SIZE)
    zero = jnp.zeros((TOKENS, WIDTH), BF16)
    one = jnp.ones((TOKENS, WIDTH), BF16)
    queries_by_head = jnp.concatenate(
        [jnp.where(head == h, queries, zero) for h in range(HEADS)], axis=0
    )
    values_by_head = jnp.concatenate(
        [jnp.where(head == h, values, zero) for h in range(HEADS)], axis=0
    )
    ones_by_head = jnp.concatenate([jnp.where(head == h, one, zero) for h in range(HEADS)], axis=0)
    scores = dot_t(queries_by_head, keys) + (keep - 1.0) * 1e9
    weights = jnp.exp(scores - jnp.max(scores, axis=-1, keepdims=True)).astype(BF16)
    weights = jnp.concatenate(
        [weights[h * TOKENS : (h + 1) * TOKENS] for h in range(HEADS)], axis=1
    )
    mixed = dot(weights, values_by_head) / dot(weights, ones_by_head)
    attended = (mixed * gates).astype(BF16)
    loads[11].wait()
    loads[12].wait()
    upd_send[...] = pack_halves(dot(attended, wo[...]) + bo[...])

    relay(REACH)
    relay(-REACH)
    lax.fori_loop(before_high, reach_high, near_send, 0)
    lax.fori_loop(0, jnp.where(quad == 1, BLOCK, 0), across_send, 0)
    send_rows(upd_send, upd_recv, upd_ssem, upd_rsem)
    lax.fori_loop(before + 1, BLOCK, near_take, 0)
    lax.fori_loop(0, jnp.where(quad == 0, BLOCK, 0), across_send, 0)
    lax.fori_loop(0, BLOCK, across_take, 0)

    pltpu.make_async_copy(upd_recv, upd_recv, upd_rsem).wait()
    by_row = (col == lax.rem(row, GROUPS) * ROWS + lax.div(row, GROUPS)).astype(F32).astype(BF16)
    update = jnp.concatenate(unpack_halves(upd_recv[...]), axis=1).astype(BF16)
    column_out[...] = dot(by_row, update).astype(BF16).reshape(ROWS, GROUPS, WIDTH)

    sent(lbuf.at[some], l_rsem)
    gap = jnp.zeros((GROUPS, ROWS, LANES), F32)
    lefts = []
    for side in range(2):
        parts = []
        for a in range(2):
            for tile in unpack_halves(lbuf[:, a]):
                rows = [tile.reshape(GROUPS, ROWS, LANES), gap]
                parts.append(
                    jnp.concatenate(rows[::-1] if side else rows, axis=1)
                    .reshape(2 * TOKENS, LANES)
                    .T
                )
        lefts.append(
            jnp.concatenate(parts, axis=0).astype(BF16).reshape(8, 4, GROUPS, 2 * TOKENS)
        )
    loads[13].wait()
    loads[14].wait()
    kept = jnp.sum(keep)

    for half in range(2):
        pltpu.make_async_copy(rbuf.at[half], rbuf.at[half], r_rsem.at[half]).wait()
    right = jnp.concatenate(
        [rbuf[half, :, a].reshape(2 * TOKENS, LANES) for half in range(2) for a in range(2)], axis=1
    )

    products = []
    for a in range(4):
        turned = [
            right[:, LANES * t : LANES * (t + 1)]
            if a == 0
            else pltpu.roll(right[:, LANES * t : LANES * (t + 1)], FACTORS * a, 1)
            for t in range(4)
        ]
        turned = jnp.concatenate(turned, axis=1)
        products.append(
            [
                dot(lefts[side][:, a].reshape(TOKENS, 2 * TOKENS), turned)
                .astype(BF16)
                .reshape(8, GROUPS, 4 * LANES)
                for side in range(2)
            ]
        )

    block = lax.div(iota((GROUPS, LANES), 1), FACTORS)
    odd, high = lax.rem(block, 2) == 1, block >= 2
    flat = [[[None] * 8 for _ in range(8)] for _ in range(4)]
    for t in range(4):
        for side in range(2):
            for c in range(8):
                v = [products[a][side][c, :, LANES * t : LANES * (t + 1)] for a in range(4)]
                even_up, even_down = jnp.where(high, v[2], v[0]), jnp.where(high, v[0], v[2])
                odd_up, odd_down = jnp.where(high, v[3], v[1]), jnp.where(high, v[1], v[3])
                place = 2 * t + side
                flat[0][place][c] = jnp.where(odd, odd_up, even_up)
                flat[1][place][c] = jnp.where(odd, even_up, odd_down)
                flat[2][place][c] = jnp.where(odd, odd_down, even_down)
                flat[3][place][c] = jnp.where(odd, even_down, odd_up)
    couple = wz[...].reshape(8, 4, FACTORS, C_Z)
    for b in range(4):
        mixing = jnp.concatenate(
            [couple[c, (g - b) % 4] for c in range(8) for g in range(4)], axis=0
        )
        sums = dot(
            jnp.concatenate([jnp.concatenate(r, axis=1) for r in flat[b]], axis=0), mixing
        )
        for place in range(8):
            total[pl.ds(4 * place + b, GROUPS, stride=2 * GROUPS), :] = sums[
                GROUPS * place : GROUPS * (place + 1)
            ]
    pair_out[...] = (total[...] / kept + bz[...]).astype(BF16).reshape(GROUPS, 2 * GROUPS, C_Z)

    sent(lbuf.at[some], l_ssem)
    sent(msa_send.at[some], msa_ssem)
    sent(upd_send.at[some], upd_ssem)

    @pl.when(quad == 3)
    def _():
        sent(zbuf.at[pl.ds(0, QUAD)], across_ssem)

    @pl.when(quad != 3)
    def _():
        sent(zbuf.at[pl.ds(0, BLOCK)], across_ssem)

    @pl.when(quad == 0)
    def _():
        sent(zbuf.at[pl.ds(0, QUAD)], far_ssem)

    def near_sent(there, _):
        @pl.when(there != z)
        def _():
            sent(zbuf.at[0], near_ssem.at[there])

        return 0

    lax.fori_loop(reach_low, reach_high, near_sent, 0)
    for i in range(1, REACH):
        up = jnp.logical_and(z - REACH >= first, z + i < last)
        down = jnp.logical_and(z + REACH < last, z - i >= first)

        @pl.when(jnp.logical_and(jnp.logical_not(early), jnp.logical_or(up, down)))
        def _():
            sent(zbuf.at[0], relay_ssem.at[i])

    sent(zbuf, r_ssem)
    sent(zbuf.at[some], r_ssem)


def store(column, pair, column_out, pair_out, sem):
    copies = [
        pltpu.make_async_copy(pair, pair_out, sem.at[0]),
        pltpu.make_async_copy(column, column_out, sem.at[1]),
    ]
    for copy in copies:
        copy.start()
    for copy in copies:
        copy.wait()


def local(
    alignment_activity,
    existing_strand_flags,
    existing_position_flags,
    asking_vector_map,
    lookup_address_map,
    content_vector_map,
    sigmoid_switch_map,
    final_mixing_map,
    final_offset_vector,
    first_factor_map,
    first_factor_offset,
    second_factor_map,
    second_factor_offset,
    couple_mixing_map,
    couple_change_offset,
):
    args = (
        alignment_activity,
        existing_strand_flags.reshape(1, -1),
        existing_position_flags.reshape(1, -1),
        asking_vector_map,
        lookup_address_map,
        content_vector_map,
        sigmoid_switch_map,
        final_mixing_map,
        final_offset_vector.reshape(1, -1),
        first_factor_map.T,
        first_factor_offset.reshape(1, -1),
        second_factor_map.T,
        second_factor_offset.reshape(1, -1),
        couple_mixing_map,
        couple_change_offset.reshape(1, -1),
    )
    piece = (2 * ROWS, LANES)
    results = pl.pallas_call(
        kernel,
        out_shape=(
            jax.ShapeDtypeStruct((ROWS, GROUPS, WIDTH), BF16),
            jax.ShapeDtypeStruct((GROUPS, 2 * GROUPS, C_Z), BF16),
        ),
        in_specs=[pl.BlockSpec(memory_space=pl.ANY)] * len(args),
        out_specs=[pl.BlockSpec(memory_space=pltpu.VMEM)] * 2,
        scratch_shapes=[pltpu.VMEM(a.shape, a.dtype) for a in args]
        + [
            pltpu.VMEM((GROUPS, *piece), BF16),
            pltpu.VMEM((GROUPS, *piece), BF16),
            pltpu.VMEM((GROUPS, *piece), BF16),
            pltpu.VMEM((GROUPS, *piece), BF16),
            pltpu.VMEM((GROUPS, 2, *piece), BF16),
            pltpu.VMEM((GROUPS, 2, *piece), BF16),
            pltpu.VMEM((2, GROUPS, 2, *piece), BF16),
            pltpu.VMEM((2 * WIDTH, C_Z), F32),
            pltpu.SemaphoreType.DMA((len(args),)),
            pltpu.SemaphoreType.DMA,
            pltpu.SemaphoreType.DMA,
            pltpu.SemaphoreType.DMA,
            pltpu.SemaphoreType.DMA,
            pltpu.SemaphoreType.DMA,
            pltpu.SemaphoreType.DMA,
            pltpu.SemaphoreType.DMA,
            pltpu.SemaphoreType.DMA,
            pltpu.SemaphoreType.DMA((GROUPS,)),
            pltpu.SemaphoreType.DMA((REACH,)),
            pltpu.SemaphoreType.DMA((GROUPS,)),
            pltpu.SemaphoreType.DMA,
            pltpu.SemaphoreType.DMA((2,)),
            pltpu.SemaphoreType.REGULAR((GROUPS,)),
        ],
        compiler_params=pltpu.CompilerParams(
            collective_id=0, has_side_effects=True, vmem_limit_bytes=16 * 1024 * 1024
        ),
        name="column_attention_and_outer_mean",
    )(*[pltpu.with_memory_space_constraint(a, pltpu.HBM) for a in args])
    return pl.pallas_call(
        store,
        out_shape=tuple(jax.ShapeDtypeStruct(r.shape, r.dtype) for r in results),
        in_specs=[pl.BlockSpec(memory_space=pltpu.VMEM)] * 2,
        out_specs=[pl.BlockSpec(memory_space=pltpu.HBM)] * 2,
        scratch_shapes=[pltpu.SemaphoreType.DMA((2,))],
        compiler_params=pltpu.CompilerParams(vmem_limit_bytes=2 * 1024 * 1024),
        name="store_results",
    )(*[pltpu.with_memory_space_constraint(r, pltpu.VMEM) for r in results])


def solution(mesh):
    return jax.shard_map(
        local,
        mesh=mesh,
        in_specs=(P("pair", "dap", None),) + (P(),) * 14,
        out_specs=(P("pair", "dap", None), P("dap", "pair", None)),
        check_vma=False,
    )
```

```python
import jax
import jax.numpy as jnp
from jax import lax
from jax.experimental import pallas as pl
from jax.experimental.pallas import tpu as pltpu
from jax.sharding import PartitionSpec as P

GROUPS = 16
ROWS = 8
TOKENS = 128
WIDTH = 256
LANES = 128
HEADS = 8
HEAD_SIZE = 32
FACTORS = 32
C_Z = 128
BLOCK = 8
QUAD = 4
SOON = 6
REACH = 4
F32 = jnp.float32
BF16 = jnp.bfloat16
MESH = pl.DeviceIdType.MESH


def iota(shape, axis):
    return lax.broadcasted_iota(jnp.int32, shape, axis)


def dot(a, b):
    return jnp.dot(a, b, preferred_element_type=F32)


def dot_t(a, b):
    return lax.dot_general(a, b, (((1,), (1,)), ((), ())), preferred_element_type=F32)


def pack_halves(wide):
    low = wide[:, :LANES].reshape(GROUPS, ROWS, LANES)
    high = wide[:, LANES:].reshape(GROUPS, ROWS, LANES)
    return jnp.concatenate([low, high], axis=1).astype(BF16)


def unpack_halves(packed):
    tall = packed.astype(F32)
    return (
        tall[:, :ROWS].reshape(TOKENS, LANES),
        tall[:, ROWS:].reshape(TOKENS, LANES),
    )


def kernel(
    x_hbm,
    strand_hbm,
    position_hbm,
    wq_hbm,
    wk_hbm,
    wv_hbm,
    wg_hbm,
    wo_hbm,
    bo_hbm,
    w1_hbm,
    b1_hbm,
    w2_hbm,
    b2_hbm,
    wz_hbm,
    bz_hbm,
    column_out,
    pair_out,
    x,
    strand,
    position,
    wq,
    wk,
    wv,
    wg,
    wo,
    bo,
    w1,
    b1,
    w2,
    b2,
    wz,
    bz,
    msa_send,
    msa_recv,
    upd_send,
    upd_recv,
    lbuf,
    zbuf,
    rbuf,
    total,
    load_sem,
    msa_ssem,
    msa_rsem,
    upd_ssem,
    upd_rsem,
    l_ssem,
    l_rsem,
    across_ssem,
    far_ssem,
    near_ssem,
    relay_ssem,
    z_rsem,
    r_ssem,
    r_rsem,
    ready,
):
    d = lax.axis_index("dap")
    q = lax.axis_index("pair")
    z = lax.div(d, 2)
    xl = lax.rem(d, 2)
    other = 1 - xl

    pairs = [
        (x_hbm, x),
        (strand_hbm, strand),
        (position_hbm, position),
        (w1_hbm, w1),
        (b1_hbm, b1),
        (w2_hbm, w2),
        (b2_hbm, b2),
        (wq_hbm, wq),
        (wk_hbm, wk),
        (wv_hbm, wv),
        (wg_hbm, wg),
        (wo_hbm, wo),
        (bo_hbm, bo),
        (wz_hbm, wz),
        (bz_hbm, bz),
    ]
    loads = [pltpu.make_async_copy(a, b, load_sem.at[i]) for i, (a, b) in enumerate(pairs)]
    loads[0].start()

    y, xh, core = lax.div(q, 4), lax.rem(lax.div(q, 2), 2), lax.rem(q, 2)
    steps = [(2, 1), (1, 1), (3, 1), (2, 0), (0, 1), (1, 0), (3, 0), (0, 0)]
    partners = [
        lax.rem(y + a, 4) * 4 + lax.rem(xh + b, 2) * 2 + lax.rem(core + e, 2)
        for a, b in steps
        for e in (0, 1)
        if a + b + e > 0
    ]

    barrier = pltpu.get_barrier_semaphore()

    def line(there):
        return (there * 2 + xl, q)

    quad = lax.div(z, QUAD)
    early = z < BLOCK
    first = jnp.where(early, 0, BLOCK)
    last = first + BLOCK
    reach = jnp.where(early, BLOCK, REACH)
    reach_low = jnp.maximum(z - reach, first)
    reach_high = jnp.minimum(z + reach + 1, last)
    before = jnp.where(early, REACH - 1, REACH)
    before_high = jnp.minimum(z + before + 1, last)
    below = jnp.where(early, 0, BLOCK)

    def greet_line(there, _):
        pl.semaphore_signal(barrier, inc=1, device_id=line(there), device_id_type=MESH)
        return 0

    def greet(there_d, there_q):
        pl.semaphore_signal(barrier, inc=1, device_id=(there_d, there_q), device_id_type=MESH)

    lax.fori_loop(z + 1, reach_high, greet_line, 0)
    lax.fori_loop(BLOCK, BLOCK + BLOCK - below, greet_line, 0)
    for there in partners:
        greet(z * 2 + other, there)
        greet(d, there)
    greet(z * 2 + other, q)

    for load in loads[1:]:
        load.start()

    loads[0].wait()
    wide = x[...].astype(F32).reshape(TOKENS, WIDTH)
    centered = wide - jnp.mean(wide, axis=-1, keepdims=True)
    spread = jnp.mean(centered * centered, axis=-1, keepdims=True)
    normed = (centered * lax.rsqrt(spread + 1e-05)).astype(BF16)

    row = iota((TOKENS, TOKENS), 0)
    col = iota((TOKENS, TOKENS), 1)
    by_residue = (col == lax.rem(row, ROWS) * GROUPS + lax.div(row, ROWS)).astype(F32).astype(BF16)
    for load in loads[1:7]:
        load.wait()
    keep = strand[...].astype(F32)
    present = position[...].astype(F32)
    keep_rows = jnp.sum(
        jnp.where(col == q * ROWS + lax.div(row, GROUPS), keep, 0.0), axis=-1, keepdims=True
    )
    row4 = iota((TOKENS, 4 * LANES), 0)
    col4 = iota((TOKENS, 4 * LANES), 1)
    residue = lax.rem(row4, GROUPS)
    keep_residues = jnp.sum(
        jnp.where(col4 == d * GROUPS + residue, present, 0.0), axis=-1, keepdims=True
    )
    both = keep_rows * keep_residues
    left = ((dot_t(normed, w1[...]) + b1[...]) * both).astype(BF16)
    right = ((dot_t(normed, w2[...]) + b2[...]) * both).astype(BF16)

    factor = iota((FACTORS, 4 * LANES), 0)
    lane = iota((FACTORS, 4 * LANES), 1)
    spread_left = (lax.div(lane, GROUPS) == factor).astype(F32).astype(BF16)
    spread_right = (lax.rem(lane, FACTORS) == factor).astype(F32).astype(BF16)
    pick_row = iota((ROWS, TOKENS), 0)
    pick_col = iota((ROWS, TOKENS), 1)
    pick = (lax.div(pick_col, GROUPS) == pick_row).astype(F32).astype(BF16)
    left_lanes = jnp.where(lax.rem(col4, GROUPS) == residue, dot(left, spread_left), 0.0)
    right_lanes = jnp.where(lax.div(col4, FACTORS) == residue, dot(right, spread_right), 0.0)
    right_rows = dot(pick, right_lanes.astype(BF16))

    def fold(rows):
        tiles = [rows[:, LANES * g : LANES * (g + 1)] for g in range(4)]
        return jnp.concatenate(tiles, axis=0).reshape(1, 2, 2 * ROWS, LANES).astype(BF16)

    zbuf[pl.ds(z, 1)] = fold(right_rows)
    msa_send[...] = pack_halves(dot(by_residue, normed))
    left_rows = dot(pick, left_lanes.astype(BF16))
    lbuf[pl.ds(q, 1)] = fold(left_rows)

    pl.semaphore_wait(barrier, 2 * GROUPS - 1 + z - reach_low + below)

    def send_piece(piece, there, sem):
        pltpu.make_async_remote_copy(
            src_ref=zbuf.at[piece],
            dst_ref=zbuf.at[piece],
            send_sem=sem,
            recv_sem=z_rsem.at[piece],
            device_id=line(there),
            device_id_type=MESH,
        ).start()

    def send_across(there, _):
        send_piece(z, there, across_ssem)
        return 0

    def send_near(there, _):
        send_piece(z, there, near_ssem.at[there])
        return 0

    def answer_line(there, _):
        pl.semaphore_signal(ready.at[z], inc=1, device_id=line(there), device_id_type=MESH)
        return 0

    def send_far_first(i, _):
        return send_across(i, 0)

    lax.fori_loop(0, jnp.where(early, 0, QUAD), send_far_first, 0)
    lax.fori_loop(reach_low, z, send_near, 0)
    lax.fori_loop(0, below, answer_line, 0)
    lax.fori_loop(reach_low, z, answer_line, 0)

    def send_rows(out, into, send_sem, recv_sem):
        for there in partners:
            pltpu.make_async_remote_copy(
                src_ref=out.at[there],
                dst_ref=into.at[q],
                send_sem=send_sem,
                recv_sem=recv_sem,
                device_id=(d, there),
                device_id_type=MESH,
            ).start()
        pltpu.make_async_copy(out.at[q], into.at[q], recv_sem).start()

    send_rows(msa_send, msa_recv, msa_ssem, msa_rsem)

    def pass_on(there):
        @pl.when(there != q)
        def _():
            pltpu.make_async_remote_copy(
                src_ref=zbuf.at[there],
                dst_ref=rbuf.at[xl, q],
                send_sem=r_ssem,
                recv_sem=r_rsem.at[xl],
                device_id=(d, there),
                device_id_type=MESH,
            ).start()

        @pl.when(there == q)
        def _():
            pltpu.make_async_copy(zbuf.at[there], rbuf.at[xl, q], r_rsem.at[xl]).start()

        pltpu.make_async_remote_copy(
            src_ref=zbuf.at[there],
            dst_ref=rbuf.at[xl, q],
            send_sem=r_ssem,
            recv_sem=r_rsem.at[xl],
            device_id=(z * 2 + other, there),
            device_id_type=MESH,
        ).start()

    pass_on(z)

    some = pl.ds(0, GROUPS - 1)

    def sent(ref, sem):
        pltpu.make_async_copy(ref, ref, sem).wait()

    def take(there):
        pltpu.make_async_copy(zbuf.at[there], zbuf.at[there], z_rsem.at[there]).wait()
        pass_on(there)

    def near_send(there, _):
        pl.semaphore_wait(ready.at[there], 1)
        return send_near(there, 0)

    def near_take(step, _):
        @pl.when(z + step < last)
        def _():
            take(z + step)

        @pl.when(z - step >= first)
        def _():
            take(z - step)

        return 0

    def relay(away):
        piece = z + away

        @pl.when(jnp.logical_and(jnp.logical_not(early), jnp.logical_and(piece >= first, piece < last)))
        def _():
            take(piece)
            for i in range(1, REACH):
                there = z - i if away > 0 else z + i

                @pl.when(jnp.logical_and(there >= first, there < last))
                def _():
                    send_piece(piece, there, relay_ssem.at[i])

    def across_send(i, _):
        there = jnp.where(quad == 0, GROUPS - 1 - i, BLOCK + i)
        pl.semaphore_wait(ready.at[there], 1)
        return send_across(there, 0)

    def across_take(i, _):
        here = i < QUAD
        piece = jnp.where(
            early,
            jnp.where(
                quad == 0,
                jnp.where(jnp.logical_or(here, z < 2), GROUPS - 1 - i, QUAD + i),
                BLOCK + i,
            ),
            jnp.where(quad == 2, BLOCK - 1 - i, i),
        )
        take(piece)

        @pl.when(jnp.logical_and(here, quad == 0))
        def _():
            send_piece(piece, z + QUAD, far_ssem)

        return 0

    lax.fori_loop(QUAD, jnp.where(quad == 2, BLOCK, QUAD), send_far_first, 0)
    lax.fori_loop(z + 1, before_high, near_send, 0)
    lax.fori_loop(1, REACH, near_take, 0)

    soon = jnp.where(jnp.logical_and(early, z >= SOON), QUAD, 0)
    lax.fori_loop(0, soon, across_send, 0)

    for load in loads[7:11]:
        load.wait()
    pltpu.make_async_copy(msa_recv, msa_recv, msa_rsem).wait()
    items = jnp.concatenate(unpack_halves(msa_recv[...]), axis=1).astype(BF16)
    queries = (dot(items, wq[...]) * HEAD_SIZE ** (-0.5)).astype(BF16)
    keys = dot(items, wk[...]).astype(BF16)
    values = dot(items, wv[...]).astype(BF16)
    gates = jax.nn.sigmoid(dot(items, wg[...]))
    head = lax.div(iota((TOKENS, WIDTH), 1), HEAD_SIZE)
    zero = jnp.zeros((TOKENS, WIDTH), BF16)
    one = jnp.ones((TOKENS, WIDTH), BF16)
    queries_by_head = jnp.concatenate(
        [jnp.where(head == h, queries, zero) for h in range(HEADS)], axis=0
    )
    values_by_head = jnp.concatenate(
        [jnp.where(head == h, values, zero) for h in range(HEADS)], axis=0
    )
    ones_by_head = jnp.concatenate([jnp.where(head == h, one, zero) for h in range(HEADS)], axis=0)
    scores = dot_t(queries_by_head, keys) + (keep - 1.0) * 1e9
    weights = jnp.exp(scores - jnp.max(scores, axis=-1, keepdims=True)).astype(BF16)
    weights = jnp.concatenate(
        [weights[h * TOKENS : (h + 1) * TOKENS] for h in range(HEADS)], axis=1
    )
    mixed = dot(weights, values_by_head) / dot(weights, ones_by_head)
    attended = (mixed * gates).astype(BF16)
    loads[11].wait()
    loads[12].wait()
    upd_send[...] = pack_halves(dot(attended, wo[...]) + bo[...])

    relay(REACH)
    relay(-REACH)
    lax.fori_loop(before_high, reach_high, near_send, 0)
    lax.fori_loop(soon, jnp.where(quad == 1, BLOCK, 0), across_send, 0)
    send_rows(upd_send, upd_recv, upd_ssem, upd_rsem)
    for there in partners:
        pltpu.make_async_remote_copy(
            src_ref=lbuf.at[q],
            dst_ref=lbuf.at[q],
            send_sem=l_ssem,
            recv_sem=l_rsem,
            device_id=(d, there),
            device_id_type=MESH,
        ).start()
    lax.fori_loop(before + 1, BLOCK, near_take, 0)
    lax.fori_loop(0, jnp.where(quad == 0, BLOCK, 0), across_send, 0)
    lax.fori_loop(0, BLOCK, across_take, 0)

    pltpu.make_async_copy(upd_recv, upd_recv, upd_rsem).wait()
    by_row = (col == lax.rem(row, GROUPS) * ROWS + lax.div(row, GROUPS)).astype(F32).astype(BF16)
    update = jnp.concatenate(unpack_halves(upd_recv[...]), axis=1).astype(BF16)
    column_out[...] = dot(by_row, update).astype(BF16).reshape(ROWS, GROUPS, WIDTH)

    sent(lbuf.at[some], l_rsem)
    gap = jnp.zeros((GROUPS, ROWS, LANES), F32)
    lefts = []
    for side in range(2):
        parts = []
        for a in range(2):
            for tile in unpack_halves(lbuf[:, a]):
                rows = [tile.reshape(GROUPS, ROWS, LANES), gap]
                parts.append(
                    jnp.concatenate(rows[::-1] if side else rows, axis=1)
                    .reshape(2 * TOKENS, LANES)
                    .T
                )
        lefts.append(
            jnp.concatenate(parts, axis=0).astype(BF16).reshape(8, 4, GROUPS, 2 * TOKENS)
        )
    loads[13].wait()
    loads[14].wait()
    kept = jnp.sum(keep)

    for half in range(2):
        pltpu.make_async_copy(rbuf.at[half], rbuf.at[half], r_rsem.at[half]).wait()
    right = jnp.concatenate(
        [rbuf[half, :, a].reshape(2 * TOKENS, LANES) for half in range(2) for a in range(2)], axis=1
    )

    products = []
    for a in range(4):
        turned = [
            right[:, LANES * t : LANES * (t + 1)]
            if a == 0
            else pltpu.roll(right[:, LANES * t : LANES * (t + 1)], FACTORS * a, 1)
            for t in range(4)
        ]
        turned = jnp.concatenate(turned, axis=1)
        products.append(
            [
                dot(lefts[side][:, a].reshape(TOKENS, 2 * TOKENS), turned)
                .astype(BF16)
                .reshape(8, GROUPS, 4 * LANES)
                for side in range(2)
            ]
        )

    block = lax.div(iota((GROUPS, LANES), 1), FACTORS)
    odd, high = lax.rem(block, 2) == 1, block >= 2
    flat = [[[None] * 8 for _ in range(8)] for _ in range(4)]
    for t in range(4):
        for side in range(2):
            for c in range(8):
                v = [products[a][side][c, :, LANES * t : LANES * (t + 1)] for a in range(4)]
                even_up, even_down = jnp.where(high, v[2], v[0]), jnp.where(high, v[0], v[2])
                odd_up, odd_down = jnp.where(high, v[3], v[1]), jnp.where(high, v[1], v[3])
                place = 2 * t + side
                flat[0][place][c] = jnp.where(odd, odd_up, even_up)
                flat[1][place][c] = jnp.where(odd, even_up, odd_down)
                flat[2][place][c] = jnp.where(odd, odd_down, even_down)
                flat[3][place][c] = jnp.where(odd, even_down, odd_up)
    couple = wz[...].reshape(8, 4, FACTORS, C_Z)
    for b in range(4):
        mixing = jnp.concatenate(
            [couple[c, (g - b) % 4] for c in range(8) for g in range(4)], axis=0
        )
        sums = dot(
            jnp.concatenate([jnp.concatenate(r, axis=1) for r in flat[b]], axis=0), mixing
        )
        for place in range(8):
            total[pl.ds(4 * place + b, GROUPS, stride=2 * GROUPS), :] = sums[
                GROUPS * place : GROUPS * (place + 1)
            ]
    pair_out[...] = (total[...] / kept + bz[...]).astype(BF16).reshape(GROUPS, 2 * GROUPS, C_Z)

    sent(lbuf.at[some], l_ssem)
    sent(msa_send.at[some], msa_ssem)
    sent(upd_send.at[some], upd_ssem)

    @pl.when(quad == 3)
    def _():
        sent(zbuf.at[pl.ds(0, QUAD)], across_ssem)

    @pl.when(quad != 3)
    def _():
        sent(zbuf.at[pl.ds(0, BLOCK)], across_ssem)

    @pl.when(quad == 0)
    def _():
        sent(zbuf.at[pl.ds(0, QUAD)], far_ssem)

    def near_sent(there, _):
        @pl.when(there != z)
        def _():
            sent(zbuf.at[0], near_ssem.at[there])

        return 0

    lax.fori_loop(reach_low, reach_high, near_sent, 0)
    for i in range(1, REACH):
        up = jnp.logical_and(z - REACH >= first, z + i < last)
        down = jnp.logical_and(z + REACH < last, z - i >= first)

        @pl.when(jnp.logical_and(jnp.logical_not(early), jnp.logical_or(up, down)))
        def _():
            sent(zbuf.at[0], relay_ssem.at[i])

    sent(zbuf, r_ssem)
    sent(zbuf.at[some], r_ssem)


def store(column, pair, column_out, pair_out, sem):
    copies = [
        pltpu.make_async_copy(pair, pair_out, sem.at[0]),
        pltpu.make_async_copy(column, column_out, sem.at[1]),
    ]
    for copy in copies:
        copy.start()
    for copy in copies:
        copy.wait()


def local(
    alignment_activity,
    existing_strand_flags,
    existing_position_flags,
    asking_vector_map,
    lookup_address_map,
    content_vector_map,
    sigmoid_switch_map,
    final_mixing_map,
    final_offset_vector,
    first_factor_map,
    first_factor_offset,
    second_factor_map,
    second_factor_offset,
    couple_mixing_map,
    couple_change_offset,
):
    args = (
        alignment_activity,
        existing_strand_flags.reshape(1, -1),
        existing_position_flags.reshape(1, -1),
        asking_vector_map,
        lookup_address_map,
        content_vector_map,
        sigmoid_switch_map,
        final_mixing_map,
        final_offset_vector.reshape(1, -1),
        first_factor_map.T,
        first_factor_offset.reshape(1, -1),
        second_factor_map.T,
        second_factor_offset.reshape(1, -1),
        couple_mixing_map,
        couple_change_offset.reshape(1, -1),
    )
    piece = (2 * ROWS, LANES)
    results = pl.pallas_call(
        kernel,
        out_shape=(
            jax.ShapeDtypeStruct((ROWS, GROUPS, WIDTH), BF16),
            jax.ShapeDtypeStruct((GROUPS, 2 * GROUPS, C_Z), BF16),
        ),
        in_specs=[pl.BlockSpec(memory_space=pl.ANY)] * len(args),
        out_specs=[pl.BlockSpec(memory_space=pltpu.VMEM)] * 2,
        scratch_shapes=[pltpu.VMEM(a.shape, a.dtype) for a in args]
        + [
            pltpu.VMEM((GROUPS, *piece), BF16),
            pltpu.VMEM((GROUPS, *piece), BF16),
            pltpu.VMEM((GROUPS, *piece), BF16),
            pltpu.VMEM((GROUPS, *piece), BF16),
            pltpu.VMEM((GROUPS, 2, *piece), BF16),
            pltpu.VMEM((GROUPS, 2, *piece), BF16),
            pltpu.VMEM((2, GROUPS, 2, *piece), BF16),
            pltpu.VMEM((2 * WIDTH, C_Z), F32),
            pltpu.SemaphoreType.DMA((len(args),)),
            pltpu.SemaphoreType.DMA,
            pltpu.SemaphoreType.DMA,
            pltpu.SemaphoreType.DMA,
            pltpu.SemaphoreType.DMA,
            pltpu.SemaphoreType.DMA,
            pltpu.SemaphoreType.DMA,
            pltpu.SemaphoreType.DMA,
            pltpu.SemaphoreType.DMA,
            pltpu.SemaphoreType.DMA((GROUPS,)),
            pltpu.SemaphoreType.DMA((REACH,)),
            pltpu.SemaphoreType.DMA((GROUPS,)),
            pltpu.SemaphoreType.DMA,
            pltpu.SemaphoreType.DMA((2,)),
            pltpu.SemaphoreType.REGULAR((GROUPS,)),
        ],
        compiler_params=pltpu.CompilerParams(
            collective_id=0, has_side_effects=True, vmem_limit_bytes=16 * 1024 * 1024
        ),
        name="column_attention_and_outer_mean",
    )(*[pltpu.with_memory_space_constraint(a, pltpu.HBM) for a in args])
    return pl.pallas_call(
        store,
        out_shape=tuple(jax.ShapeDtypeStruct(r.shape, r.dtype) for r in results),
        in_specs=[pl.BlockSpec(memory_space=pltpu.VMEM)] * 2,
        out_specs=[pl.BlockSpec(memory_space=pltpu.HBM)] * 2,
        scratch_shapes=[pltpu.SemaphoreType.DMA((2,))],
        compiler_params=pltpu.CompilerParams(vmem_limit_bytes=2 * 1024 * 1024),
        name="store_results",
    )(*[pltpu.with_memory_space_constraint(r, pltpu.VMEM) for r in results])


def solution(mesh):
    return jax.shard_map(
        local,
        mesh=mesh,
        in_specs=(P("pair", "dap", None),) + (P(),) * 14,
        out_specs=(P("pair", "dap", None), P("dap", "pair", None)),
        check_vma=False,
    )
```

```python
import jax
import jax.numpy as jnp
from jax import lax
from jax.experimental import pallas as pl
from jax.experimental.pallas import tpu as pltpu
from jax.sharding import PartitionSpec as P

GROUPS = 16
ROWS = 8
TOKENS = 128
WIDTH = 256
LANES = 128
HEADS = 8
HEAD_SIZE = 32
FACTORS = 32
C_Z = 128
BLOCK = 8
QUAD = 4
SOON = 6
REACH = 4
F32 = jnp.float32
BF16 = jnp.bfloat16
MESH = pl.DeviceIdType.MESH


def iota(shape, axis):
    return lax.broadcasted_iota(jnp.int32, shape, axis)


def dot(a, b):
    return jnp.dot(a, b, preferred_element_type=F32)


def dot_t(a, b):
    return lax.dot_general(a, b, (((1,), (1,)), ((), ())), preferred_element_type=F32)


def pack_halves(wide):
    low = wide[:, :LANES].reshape(GROUPS, ROWS, LANES)
    high = wide[:, LANES:].reshape(GROUPS, ROWS, LANES)
    return jnp.concatenate([low, high], axis=1).astype(BF16)


def unpack_halves(packed):
    tall = packed.astype(F32)
    return (
        tall[:, :ROWS].reshape(TOKENS, LANES),
        tall[:, ROWS:].reshape(TOKENS, LANES),
    )


def kernel(
    x_hbm,
    strand_hbm,
    position_hbm,
    wq_hbm,
    wk_hbm,
    wv_hbm,
    wg_hbm,
    wo_hbm,
    bo_hbm,
    w1_hbm,
    b1_hbm,
    w2_hbm,
    b2_hbm,
    wz_hbm,
    bz_hbm,
    column_out,
    pair_out,
    x,
    strand,
    position,
    wq,
    wk,
    wv,
    wg,
    wo,
    bo,
    w1,
    b1,
    w2,
    b2,
    wz,
    bz,
    msa_send,
    msa_recv,
    upd_send,
    upd_recv,
    lbuf,
    zbuf,
    rbuf,
    total,
    load_sem,
    msa_ssem,
    msa_rsem,
    upd_ssem,
    upd_rsem,
    l_ssem,
    l_rsem,
    across_ssem,
    far_ssem,
    near_ssem,
    relay_ssem,
    z_rsem,
    r_ssem,
    r_rsem,
    ready,
):
    d = lax.axis_index("dap")
    q = lax.axis_index("pair")
    z = lax.div(d, 2)
    xl = lax.rem(d, 2)
    other = 1 - xl

    pairs = [
        (x_hbm, x),
        (strand_hbm, strand),
        (position_hbm, position),
        (w1_hbm, w1),
        (b1_hbm, b1),
        (w2_hbm, w2),
        (b2_hbm, b2),
        (wq_hbm, wq),
        (wk_hbm, wk),
        (wv_hbm, wv),
        (wg_hbm, wg),
        (wo_hbm, wo),
        (bo_hbm, bo),
        (wz_hbm, wz),
        (bz_hbm, bz),
    ]
    loads = [pltpu.make_async_copy(a, b, load_sem.at[i]) for i, (a, b) in enumerate(pairs)]
    for load in loads[:7]:
        load.start()

    y, xh, core = lax.div(q, 4), lax.rem(lax.div(q, 2), 2), lax.rem(q, 2)
    steps = [(2, 1), (1, 1), (3, 1), (2, 0), (0, 1), (1, 0), (3, 0), (0, 0)]
    partners = [
        lax.rem(y + a, 4) * 4 + lax.rem(xh + b, 2) * 2 + lax.rem(core + e, 2)
        for a, b in steps
        for e in (0, 1)
        if a + b + e > 0
    ]

    barrier = pltpu.get_barrier_semaphore()

    def line(there):
        return (there * 2 + xl, q)

    quad = lax.div(z, QUAD)
    early = z < BLOCK
    first = jnp.where(early, 0, BLOCK)
    last = first + BLOCK
    reach = jnp.where(early, BLOCK, REACH)
    reach_low = jnp.maximum(z - reach, first)
    reach_high = jnp.minimum(z + reach + 1, last)
    before = jnp.where(early, REACH - 1, REACH)
    before_high = jnp.minimum(z + before + 1, last)
    below = jnp.where(early, 0, BLOCK)

    def greet_line(there, _):
        pl.semaphore_signal(barrier, inc=1, device_id=line(there), device_id_type=MESH)
        return 0

    def greet(there_d, there_q):
        pl.semaphore_signal(barrier, inc=1, device_id=(there_d, there_q), device_id_type=MESH)

    lax.fori_loop(z + 1, reach_high, greet_line, 0)
    lax.fori_loop(BLOCK, BLOCK + BLOCK - below, greet_line, 0)
    for there in partners:
        greet(z * 2 + other, there)
        greet(d, there)
    greet(z * 2 + other, q)

    for load in loads[7:]:
        load.start()

    loads[0].wait()
    wide = x[...].astype(F32).reshape(TOKENS, WIDTH)
    centered = wide - jnp.mean(wide, axis=-1, keepdims=True)
    spread = jnp.mean(centered * centered, axis=-1, keepdims=True)
    normed = (centered * lax.rsqrt(spread + 1e-05)).astype(BF16)

    row = iota((TOKENS, TOKENS), 0)
    col = iota((TOKENS, TOKENS), 1)
    by_residue = (col == lax.rem(row, ROWS) * GROUPS + lax.div(row, ROWS)).astype(F32).astype(BF16)
    for load in loads[1:7]:
        load.wait()
    keep = strand[...].astype(F32)
    present = position[...].astype(F32)
    keep_rows = jnp.sum(
        jnp.where(col == q * ROWS + lax.div(row, GROUPS), keep, 0.0), axis=-1, keepdims=True
    )
    row4 = iota((TOKENS, 4 * LANES), 0)
    col4 = iota((TOKENS, 4 * LANES), 1)
    residue = lax.rem(row4, GROUPS)
    keep_residues = jnp.sum(
        jnp.where(col4 == d * GROUPS + residue, present, 0.0), axis=-1, keepdims=True
    )
    both = keep_rows * keep_residues
    left = ((dot_t(normed, w1[...]) + b1[...]) * both).astype(BF16)
    right = ((dot_t(normed, w2[...]) + b2[...]) * both).astype(BF16)

    factor = iota((FACTORS, 4 * LANES), 0)
    lane = iota((FACTORS, 4 * LANES), 1)
    spread_left = (lax.div(lane, GROUPS) == factor).astype(F32).astype(BF16)
    spread_right = (lax.rem(lane, FACTORS) == factor).astype(F32).astype(BF16)
    pick_row = iota((ROWS, TOKENS), 0)
    pick_col = iota((ROWS, TOKENS), 1)
    pick = (lax.div(pick_col, GROUPS) == pick_row).astype(F32).astype(BF16)
    left_lanes = jnp.where(lax.rem(col4, GROUPS) == residue, dot(left, spread_left), 0.0)
    right_lanes = jnp.where(lax.div(col4, FACTORS) == residue, dot(right, spread_right), 0.0)
    right_rows = dot(pick, right_lanes.astype(BF16))

    def fold(rows):
        tiles = [rows[:, LANES * g : LANES * (g + 1)] for g in range(4)]
        return jnp.concatenate(tiles, axis=0).reshape(1, 2, 2 * ROWS, LANES).astype(BF16)

    zbuf[pl.ds(z, 1)] = fold(right_rows)
    msa_send[...] = pack_halves(dot(by_residue, normed))
    left_rows = dot(pick, left_lanes.astype(BF16))
    lbuf[pl.ds(q, 1)] = fold(left_rows)

    pl.semaphore_wait(barrier, 2 * GROUPS - 1 + z - reach_low + below)

    def send_piece(piece, there, sem):
        pltpu.make_async_remote_copy(
            src_ref=zbuf.at[piece],
            dst_ref=zbuf.at[piece],
            send_sem=sem,
            recv_sem=z_rsem.at[piece],
            device_id=line(there),
            device_id_type=MESH,
        ).start()

    def send_across(there, _):
        send_piece(z, there, across_ssem)
        return 0

    def send_near(there, _):
        send_piece(z, there, near_ssem.at[there])
        return 0

    def answer_line(there, _):
        pl.semaphore_signal(ready.at[z], inc=1, device_id=line(there), device_id_type=MESH)
        return 0

    lax.fori_loop(0, jnp.where(early, 0, QUAD), send_across, 0)
    lax.fori_loop(reach_low, z, send_near, 0)
    lax.fori_loop(0, below, answer_line, 0)
    lax.fori_loop(reach_low, z, answer_line, 0)

    def send_rows(out, into, send_sem, recv_sem):
        for there in partners:
            pltpu.make_async_remote_copy(
                src_ref=out.at[there],
                dst_ref=into.at[q],
                send_sem=send_sem,
                recv_sem=recv_sem,
                device_id=(d, there),
                device_id_type=MESH,
            ).start()
        pltpu.make_async_copy(out.at[q], into.at[q], recv_sem).start()

    send_rows(msa_send, msa_recv, msa_ssem, msa_rsem)

    def pass_on(there):
        @pl.when(there != q)
        def _():
            pltpu.make_async_remote_copy(
                src_ref=zbuf.at[there],
                dst_ref=rbuf.at[xl, q],
                send_sem=r_ssem,
                recv_sem=r_rsem.at[xl],
                device_id=(d, there),
                device_id_type=MESH,
            ).start()

        @pl.when(there == q)
        def _():
            pltpu.make_async_copy(zbuf.at[there], rbuf.at[xl, q], r_rsem.at[xl]).start()

        pltpu.make_async_remote_copy(
            src_ref=zbuf.at[there],
            dst_ref=rbuf.at[xl, q],
            send_sem=r_ssem,
            recv_sem=r_rsem.at[xl],
            device_id=(z * 2 + other, there),
            device_id_type=MESH,
        ).start()

    pass_on(z)

    some = pl.ds(0, GROUPS - 1)

    def sent(ref, sem):
        pltpu.make_async_copy(ref, ref, sem).wait()

    def take(there):
        pltpu.make_async_copy(zbuf.at[there], zbuf.at[there], z_rsem.at[there]).wait()
        pass_on(there)

    def near_send(there, _):
        pl.semaphore_wait(ready.at[there], 1)
        return send_near(there, 0)

    def near_take(step, _):
        @pl.when(z + step < last)
        def _():
            take(z + step)

        @pl.when(z - step >= first)
        def _():
            take(z - step)

        return 0

    def relay(away):
        piece = z + away

        @pl.when(jnp.logical_and(jnp.logical_not(early), jnp.logical_and(piece >= first, piece < last)))
        def _():
            take(piece)
            for i in range(1, REACH):
                there = z - i if away > 0 else z + i

                @pl.when(jnp.logical_and(there >= first, there < last))
                def _():
                    send_piece(piece, there, relay_ssem.at[i])

    def across_send(i, _):
        there = jnp.where(quad == 0, GROUPS - 1 - i, BLOCK + i)
        pl.semaphore_wait(ready.at[there], 1)
        return send_across(there, 0)

    def across_take(i, _):
        here = i < QUAD
        piece = jnp.where(
            early,
            jnp.where(
                quad == 0,
                jnp.where(jnp.logical_or(here, z < 2), GROUPS - 1 - i, QUAD + i),
                BLOCK + i,
            ),
            jnp.where(quad == 2, BLOCK - 1 - i, i),
        )
        take(piece)

        @pl.when(jnp.logical_and(here, quad == 0))
        def _():
            send_piece(piece, z + QUAD, far_ssem)

        return 0

    lax.fori_loop(QUAD, jnp.where(quad == 2, BLOCK, QUAD), send_across, 0)
    lax.fori_loop(z + 1, before_high, near_send, 0)
    lax.fori_loop(1, REACH, near_take, 0)

    soon = jnp.where(jnp.logical_and(early, z >= SOON), QUAD, 0)
    lax.fori_loop(0, soon, across_send, 0)

    for load in loads[7:11]:
        load.wait()
    pltpu.make_async_copy(msa_recv, msa_recv, msa_rsem).wait()
    items = jnp.concatenate(unpack_halves(msa_recv[...]), axis=1).astype(BF16)
    queries = (dot(items, wq[...]) * HEAD_SIZE ** (-0.5)).astype(BF16)
    keys = dot(items, wk[...]).astype(BF16)
    values = dot(items, wv[...]).astype(BF16)
    gates = jax.nn.sigmoid(dot(items, wg[...]))
    head = lax.div(iota((TOKENS, WIDTH), 1), HEAD_SIZE)
    zero = jnp.zeros((TOKENS, WIDTH), BF16)
    one = jnp.ones((TOKENS, WIDTH), BF16)
    queries_by_head = jnp.concatenate(
        [jnp.where(head == h, queries, zero) for h in range(HEADS)], axis=0
    )
    values_by_head = jnp.concatenate(
        [jnp.where(head == h, values, zero) for h in range(HEADS)], axis=0
    )
    ones_by_head = jnp.concatenate([jnp.where(head == h, one, zero) for h in range(HEADS)], axis=0)
    scores = dot_t(queries_by_head, keys) + (keep - 1.0) * 1e9
    weights = jnp.exp(scores - jnp.max(scores, axis=-1, keepdims=True)).astype(BF16)
    weights = jnp.concatenate(
        [weights[h * TOKENS : (h + 1) * TOKENS] for h in range(HEADS)], axis=1
    )
    mixed = dot(weights, values_by_head) / dot(weights, ones_by_head)
    attended = (mixed * gates).astype(BF16)
    loads[11].wait()
    loads[12].wait()
    upd_send[...] = pack_halves(dot(attended, wo[...]) + bo[...])

    relay(REACH)
    relay(-REACH)
    lax.fori_loop(before_high, reach_high, near_send, 0)
    lax.fori_loop(soon, jnp.where(quad == 1, BLOCK, 0), across_send, 0)
    send_rows(upd_send, upd_recv, upd_ssem, upd_rsem)
    for there in partners:
        pltpu.make_async_remote_copy(
            src_ref=lbuf.at[q],
            dst_ref=lbuf.at[q],
            send_sem=l_ssem,
            recv_sem=l_rsem,
            device_id=(d, there),
            device_id_type=MESH,
        ).start()
    lax.fori_loop(before + 1, BLOCK, near_take, 0)
    lax.fori_loop(0, jnp.where(quad == 0, BLOCK, 0), across_send, 0)
    lax.fori_loop(0, BLOCK, across_take, 0)

    pltpu.make_async_copy(upd_recv, upd_recv, upd_rsem).wait()
    by_row = (col == lax.rem(row, GROUPS) * ROWS + lax.div(row, GROUPS)).astype(F32).astype(BF16)
    update = jnp.concatenate(unpack_halves(upd_recv[...]), axis=1).astype(BF16)
    column_out[...] = dot(by_row, update).astype(BF16).reshape(ROWS, GROUPS, WIDTH)

    sent(lbuf.at[some], l_rsem)
    gap = jnp.zeros((GROUPS, ROWS, LANES), F32)
    lefts = []
    for side in range(2):
        parts = []
        for a in range(2):
            for tile in unpack_halves(lbuf[:, a]):
                rows = [tile.reshape(GROUPS, ROWS, LANES), gap]
                parts.append(
                    jnp.concatenate(rows[::-1] if side else rows, axis=1)
                    .reshape(2 * TOKENS, LANES)
                    .T
                )
        lefts.append(
            jnp.concatenate(parts, axis=0).astype(BF16).reshape(8, 4, GROUPS, 2 * TOKENS)
        )
    loads[13].wait()
    loads[14].wait()
    kept = jnp.sum(keep)

    for half in range(2):
        pltpu.make_async_copy(rbuf.at[half], rbuf.at[half], r_rsem.at[half]).wait()
    right = jnp.concatenate(
        [rbuf[half, :, a].reshape(2 * TOKENS, LANES) for half in range(2) for a in range(2)], axis=1
    )

    products = []
    for a in range(4):
        turned = [
            right[:, LANES * t : LANES * (t + 1)]
            if a == 0
            else pltpu.roll(right[:, LANES * t : LANES * (t + 1)], FACTORS * a, 1)
            for t in range(4)
        ]
        turned = jnp.concatenate(turned, axis=1)
        products.append(
            [
                dot(lefts[side][:, a].reshape(TOKENS, 2 * TOKENS), turned)
                .astype(BF16)
                .reshape(8, GROUPS, 4 * LANES)
                for side in range(2)
            ]
        )

    block = lax.div(iota((GROUPS, LANES), 1), FACTORS)
    odd, high = lax.rem(block, 2) == 1, block >= 2
    flat = [[[None] * 8 for _ in range(8)] for _ in range(4)]
    for t in range(4):
        for side in range(2):
            for c in range(8):
                v = [products[a][side][c, :, LANES * t : LANES * (t + 1)] for a in range(4)]
                even_up, even_down = jnp.where(high, v[2], v[0]), jnp.where(high, v[0], v[2])
                odd_up, odd_down = jnp.where(high, v[3], v[1]), jnp.where(high, v[1], v[3])
                place = 2 * t + side
                flat[0][place][c] = jnp.where(odd, odd_up, even_up)
                flat[1][place][c] = jnp.where(odd, even_up, odd_down)
                flat[2][place][c] = jnp.where(odd, odd_down, even_down)
                flat[3][place][c] = jnp.where(odd, even_down, odd_up)
    couple = wz[...].reshape(8, 4, FACTORS, C_Z)
    for b in range(4):
        mixing = jnp.concatenate(
            [couple[c, (g - b) % 4] for c in range(8) for g in range(4)], axis=0
        )
        sums = dot(
            jnp.concatenate([jnp.concatenate(r, axis=1) for r in flat[b]], axis=0), mixing
        )
        for place in range(8):
            total[pl.ds(4 * place + b, GROUPS, stride=2 * GROUPS), :] = sums[
                GROUPS * place : GROUPS * (place + 1)
            ]
    pair_out[...] = (total[...] / kept + bz[...]).astype(BF16).reshape(GROUPS, 2 * GROUPS, C_Z)

    sent(lbuf.at[some], l_ssem)
    sent(msa_send.at[some], msa_ssem)
    sent(upd_send.at[some], upd_ssem)

    @pl.when(quad == 3)
    def _():
        sent(zbuf.at[pl.ds(0, QUAD)], across_ssem)

    @pl.when(quad != 3)
    def _():
        sent(zbuf.at[pl.ds(0, BLOCK)], across_ssem)

    @pl.when(quad == 0)
    def _():
        sent(zbuf.at[pl.ds(0, QUAD)], far_ssem)

    def near_sent(there, _):
        @pl.when(there != z)
        def _():
            sent(zbuf.at[0], near_ssem.at[there])

        return 0

    lax.fori_loop(reach_low, reach_high, near_sent, 0)
    for i in range(1, REACH):
        up = jnp.logical_and(z - REACH >= first, z + i < last)
        down = jnp.logical_and(z + REACH < last, z - i >= first)

        @pl.when(jnp.logical_and(jnp.logical_not(early), jnp.logical_or(up, down)))
        def _():
            sent(zbuf.at[0], relay_ssem.at[i])

    sent(zbuf, r_ssem)
    sent(zbuf.at[some], r_ssem)


def store(column, pair, column_out, pair_out, sem):
    copies = [
        pltpu.make_async_copy(pair, pair_out, sem.at[0]),
        pltpu.make_async_copy(column, column_out, sem.at[1]),
    ]
    for copy in copies:
        copy.start()
    for copy in copies:
        copy.wait()


def local(
    alignment_activity,
    existing_strand_flags,
    existing_position_flags,
    asking_vector_map,
    lookup_address_map,
    content_vector_map,
    sigmoid_switch_map,
    final_mixing_map,
    final_offset_vector,
    first_factor_map,
    first_factor_offset,
    second_factor_map,
    second_factor_offset,
    couple_mixing_map,
    couple_change_offset,
):
    args = (
        alignment_activity,
        existing_strand_flags.reshape(1, -1),
        existing_position_flags.reshape(1, -1),
        asking_vector_map,
        lookup_address_map,
        content_vector_map,
        sigmoid_switch_map,
        final_mixing_map,
        final_offset_vector.reshape(1, -1),
        first_factor_map.T,
        first_factor_offset.reshape(1, -1),
        second_factor_map.T,
        second_factor_offset.reshape(1, -1),
        couple_mixing_map,
        couple_change_offset.reshape(1, -1),
    )
    piece = (2 * ROWS, LANES)
    results = pl.pallas_call(
        kernel,
        out_shape=(
            jax.ShapeDtypeStruct((ROWS, GROUPS, WIDTH), BF16),
            jax.ShapeDtypeStruct((GROUPS, 2 * GROUPS, C_Z), BF16),
        ),
        in_specs=[pl.BlockSpec(memory_space=pl.ANY)] * len(args),
        out_specs=[pl.BlockSpec(memory_space=pltpu.VMEM)] * 2,
        scratch_shapes=[pltpu.VMEM(a.shape, a.dtype) for a in args]
        + [
            pltpu.VMEM((GROUPS, *piece), BF16),
            pltpu.VMEM((GROUPS, *piece), BF16),
            pltpu.VMEM((GROUPS, *piece), BF16),
            pltpu.VMEM((GROUPS, *piece), BF16),
            pltpu.VMEM((GROUPS, 2, *piece), BF16),
            pltpu.VMEM((GROUPS, 2, *piece), BF16),
            pltpu.VMEM((2, GROUPS, 2, *piece), BF16),
            pltpu.VMEM((2 * WIDTH, C_Z), F32),
            pltpu.SemaphoreType.DMA((len(args),)),
            pltpu.SemaphoreType.DMA,
            pltpu.SemaphoreType.DMA,
            pltpu.SemaphoreType.DMA,
            pltpu.SemaphoreType.DMA,
            pltpu.SemaphoreType.DMA,
            pltpu.SemaphoreType.DMA,
            pltpu.SemaphoreType.DMA,
            pltpu.SemaphoreType.DMA,
            pltpu.SemaphoreType.DMA((GROUPS,)),
            pltpu.SemaphoreType.DMA((REACH,)),
            pltpu.SemaphoreType.DMA((GROUPS,)),
            pltpu.SemaphoreType.DMA,
            pltpu.SemaphoreType.DMA((2,)),
            pltpu.SemaphoreType.REGULAR((GROUPS,)),
        ],
        compiler_params=pltpu.CompilerParams(
            collective_id=0, has_side_effects=True, vmem_limit_bytes=16 * 1024 * 1024
        ),
        name="column_attention_and_outer_mean",
    )(*[pltpu.with_memory_space_constraint(a, pltpu.HBM) for a in args])
    return pl.pallas_call(
        store,
        out_shape=tuple(jax.ShapeDtypeStruct(r.shape, r.dtype) for r in results),
        in_specs=[pl.BlockSpec(memory_space=pltpu.VMEM)] * 2,
        out_specs=[pl.BlockSpec(memory_space=pltpu.HBM)] * 2,
        scratch_shapes=[pltpu.SemaphoreType.DMA((2,))],
        compiler_params=pltpu.CompilerParams(vmem_limit_bytes=2 * 1024 * 1024),
        name="store_results",
    )(*[pltpu.with_memory_space_constraint(r, pltpu.VMEM) for r in results])


def solution(mesh):
    return jax.shard_map(
        local,
        mesh=mesh,
        in_specs=(P("pair", "dap", None),) + (P(),) * 14,
        out_specs=(P("pair", "dap", None), P("dap", "pair", None)),
        check_vma=False,
    )
```

```python
import jax
import jax.numpy as jnp
from jax import lax
from jax.experimental import pallas as pl
from jax.experimental.pallas import tpu as pltpu
from jax.sharding import PartitionSpec as P

GROUPS = 16
ROWS = 8
TOKENS = 128
WIDTH = 256
LANES = 128
HEADS = 8
HEAD_SIZE = 32
FACTORS = 32
C_Z = 128
BLOCK = 8
QUAD = 4
SOON = 6
REACH = 4
F32 = jnp.float32
BF16 = jnp.bfloat16
MESH = pl.DeviceIdType.MESH


def iota(shape, axis):
    return lax.broadcasted_iota(jnp.int32, shape, axis)


def dot(a, b):
    return jnp.dot(a, b, preferred_element_type=F32)


def dot_t(a, b):
    return lax.dot_general(a, b, (((1,), (1,)), ((), ())), preferred_element_type=F32)


def pack_halves(wide):
    low = wide[:, :LANES].reshape(GROUPS, ROWS, LANES)
    high = wide[:, LANES:].reshape(GROUPS, ROWS, LANES)
    return jnp.concatenate([low, high], axis=1).astype(BF16)


def unpack_halves(packed):
    tall = packed.astype(F32)
    return (
        tall[:, :ROWS].reshape(TOKENS, LANES),
        tall[:, ROWS:].reshape(TOKENS, LANES),
    )


def kernel(
    x_hbm,
    strand_hbm,
    position_hbm,
    wq_hbm,
    wk_hbm,
    wv_hbm,
    wg_hbm,
    wo_hbm,
    bo_hbm,
    w1_hbm,
    b1_hbm,
    w2_hbm,
    b2_hbm,
    wz_hbm,
    bz_hbm,
    column_out,
    pair_out,
    x,
    strand,
    position,
    wq,
    wk,
    wv,
    wg,
    wo,
    bo,
    w1,
    b1,
    w2,
    b2,
    wz,
    bz,
    msa_send,
    msa_recv,
    upd_send,
    upd_recv,
    lbuf,
    zbuf,
    rbuf,
    total,
    load_sem,
    msa_ssem,
    msa_rsem,
    upd_ssem,
    upd_rsem,
    l_ssem,
    l_rsem,
    across_ssem,
    far_ssem,
    near_ssem,
    relay_ssem,
    z_rsem,
    r_ssem,
    r_rsem,
    ready,
):
    d = lax.axis_index("dap")
    q = lax.axis_index("pair")
    z = lax.div(d, 2)
    xl = lax.rem(d, 2)
    other = 1 - xl

    pairs = [
        (x_hbm, x),
        (strand_hbm, strand),
        (position_hbm, position),
        (w1_hbm, w1),
        (b1_hbm, b1),
        (w2_hbm, w2),
        (b2_hbm, b2),
        (wq_hbm, wq),
        (wk_hbm, wk),
        (wv_hbm, wv),
        (wg_hbm, wg),
        (wo_hbm, wo),
        (bo_hbm, bo),
        (wz_hbm, wz),
        (bz_hbm, bz),
    ]
    loads = [pltpu.make_async_copy(a, b, load_sem.at[i]) for i, (a, b) in enumerate(pairs)]
    for load in loads[:7]:
        load.start()

    y, xh, core = lax.div(q, 4), lax.rem(lax.div(q, 2), 2), lax.rem(q, 2)
    steps = [(2, 1), (1, 1), (3, 1), (2, 0), (0, 1), (1, 0), (3, 0), (0, 0)]
    partners = [
        lax.rem(y + a, 4) * 4 + lax.rem(xh + b, 2) * 2 + lax.rem(core + e, 2)
        for a, b in steps
        for e in (0, 1)
        if a + b + e > 0
    ]

    barrier = pltpu.get_barrier_semaphore()

    def line(there):
        return (there * 2 + xl, q)

    quad = lax.div(z, QUAD)
    early = z < BLOCK
    first = jnp.where(early, 0, BLOCK)
    last = first + BLOCK
    reach = jnp.where(early, BLOCK, REACH)
    reach_low = jnp.maximum(z - reach, first)
    reach_high = jnp.minimum(z + reach + 1, last)
    before = jnp.where(early, REACH - 1, REACH)
    before_high = jnp.minimum(z + before + 1, last)
    below = jnp.where(early, 0, BLOCK)

    def greet_line(there, _):
        pl.semaphore_signal(barrier, inc=1, device_id=line(there), device_id_type=MESH)
        return 0

    def greet(there_d, there_q):
        pl.semaphore_signal(barrier, inc=1, device_id=(there_d, there_q), device_id_type=MESH)

    lax.fori_loop(z + 1, reach_high, greet_line, 0)
    lax.fori_loop(BLOCK, BLOCK + BLOCK - below, greet_line, 0)
    for there in partners:
        greet(z * 2 + other, there)
        greet(d, there)
    greet(z * 2 + other, q)

    for load in loads[7:]:
        load.start()

    loads[0].wait()
    wide = x[...].astype(F32).reshape(TOKENS, WIDTH)
    centered = wide - jnp.mean(wide, axis=-1, keepdims=True)
    spread = jnp.mean(centered * centered, axis=-1, keepdims=True)
    normed = (centered * lax.rsqrt(spread + 1e-05)).astype(BF16)

    row = iota((TOKENS, TOKENS), 0)
    col = iota((TOKENS, TOKENS), 1)
    by_residue = (col == lax.rem(row, ROWS) * GROUPS + lax.div(row, ROWS)).astype(F32).astype(BF16)
    for load in loads[1:7]:
        load.wait()
    keep = strand[...].astype(F32)
    present = position[...].astype(F32)
    keep_rows = jnp.sum(
        jnp.where(col == q * ROWS + lax.div(row, GROUPS), keep, 0.0), axis=-1, keepdims=True
    )
    row4 = iota((TOKENS, 4 * LANES), 0)
    col4 = iota((TOKENS, 4 * LANES), 1)
    residue = lax.rem(row4, GROUPS)
    keep_residues = jnp.sum(
        jnp.where(col4 == d * GROUPS + residue, present, 0.0), axis=-1, keepdims=True
    )
    both = keep_rows * keep_residues
    left = ((dot_t(normed, w1[...]) + b1[...]) * both).astype(BF16)
    right = dot_t(normed, jnp.concatenate([w2[...]] * GROUPS, axis=0))
    right = ((right + jnp.concatenate([b2[...]] * GROUPS, axis=1)) * both).astype(BF16).astype(F32)

    factor = iota((FACTORS, 4 * LANES), 0)
    lane = iota((FACTORS, 4 * LANES), 1)
    spread_left = (lax.div(lane, GROUPS) == factor).astype(F32).astype(BF16)
    pick_row = iota((ROWS, TOKENS), 0)
    pick_col = iota((ROWS, TOKENS), 1)
    pick = (lax.div(pick_col, GROUPS) == pick_row).astype(F32).astype(BF16)
    left_lanes = jnp.where(lax.rem(col4, GROUPS) == residue, dot(left, spread_left), 0.0)
    right_lanes = jnp.where(lax.div(col4, FACTORS) == residue, right, 0.0)
    right_rows = dot(pick, right_lanes.astype(BF16))

    def fold(rows):
        tiles = [rows[:, LANES * g : LANES * (g + 1)] for g in range(4)]
        return jnp.concatenate(tiles, axis=0).reshape(1, 2, 2 * ROWS, LANES).astype(BF16)

    zbuf[pl.ds(z, 1)] = fold(right_rows)
    msa_send[...] = pack_halves(dot(by_residue, normed))
    left_rows = dot(pick, left_lanes.astype(BF16))
    lbuf[pl.ds(q, 1)] = fold(left_rows)

    pl.semaphore_wait(barrier, 2 * GROUPS - 1 + z - reach_low + below)

    def send_piece(piece, there, sem):
        pltpu.make_async_remote_copy(
            src_ref=zbuf.at[piece],
            dst_ref=zbuf.at[piece],
            send_sem=sem,
            recv_sem=z_rsem.at[piece],
            device_id=line(there),
            device_id_type=MESH,
        ).start()

    def send_across(there, _):
        send_piece(z, there, across_ssem)
        return 0

    def send_near(there, _):
        send_piece(z, there, near_ssem.at[there])
        return 0

    def answer_line(there, _):
        pl.semaphore_signal(ready.at[z], inc=1, device_id=line(there), device_id_type=MESH)
        return 0

    lax.fori_loop(0, jnp.where(early, 0, QUAD), send_across, 0)
    lax.fori_loop(reach_low, z, send_near, 0)
    lax.fori_loop(0, below, answer_line, 0)
    lax.fori_loop(reach_low, z, answer_line, 0)

    def send_rows(out, into, send_sem, recv_sem):
        for there in partners:
            pltpu.make_async_remote_copy(
                src_ref=out.at[there],
                dst_ref=into.at[q],
                send_sem=send_sem,
                recv_sem=recv_sem,
                device_id=(d, there),
                device_id_type=MESH,
            ).start()
        pltpu.make_async_copy(out.at[q], into.at[q], recv_sem).start()

    send_rows(msa_send, msa_recv, msa_ssem, msa_rsem)

    def pass_on(there):
        @pl.when(there != q)
        def _():
            pltpu.make_async_remote_copy(
                src_ref=zbuf.at[there],
                dst_ref=rbuf.at[xl, q],
                send_sem=r_ssem,
                recv_sem=r_rsem.at[xl],
                device_id=(d, there),
                device_id_type=MESH,
            ).start()

        @pl.when(there == q)
        def _():
            pltpu.make_async_copy(zbuf.at[there], rbuf.at[xl, q], r_rsem.at[xl]).start()

        pltpu.make_async_remote_copy(
            src_ref=zbuf.at[there],
            dst_ref=rbuf.at[xl, q],
            send_sem=r_ssem,
            recv_sem=r_rsem.at[xl],
            device_id=(z * 2 + other, there),
            device_id_type=MESH,
        ).start()

    pass_on(z)

    some = pl.ds(0, GROUPS - 1)

    def sent(ref, sem):
        pltpu.make_async_copy(ref, ref, sem).wait()

    def take(there):
        pltpu.make_async_copy(zbuf.at[there], zbuf.at[there], z_rsem.at[there]).wait()
        pass_on(there)

    def near_send(there, _):
        pl.semaphore_wait(ready.at[there], 1)
        return send_near(there, 0)

    def near_take(step, _):
        @pl.when(z + step < last)
        def _():
            take(z + step)

        @pl.when(z - step >= first)
        def _():
            take(z - step)

        return 0

    def relay(away):
        piece = z + away

        @pl.when(jnp.logical_and(jnp.logical_not(early), jnp.logical_and(piece >= first, piece < last)))
        def _():
            take(piece)
            for i in range(1, REACH):
                there = z - i if away > 0 else z + i

                @pl.when(jnp.logical_and(there >= first, there < last))
                def _():
                    send_piece(piece, there, relay_ssem.at[i])

    def across_send(i, _):
        there = jnp.where(quad == 0, GROUPS - 1 - i, BLOCK + i)
        pl.semaphore_wait(ready.at[there], 1)
        return send_across(there, 0)

    def across_take(i, _):
        here = i < QUAD
        piece = jnp.where(
            early,
            jnp.where(
                quad == 0,
                jnp.where(jnp.logical_or(here, z < 2), GROUPS - 1 - i, QUAD + i),
                BLOCK + i,
            ),
            jnp.where(quad == 2, BLOCK - 1 - i, i),
        )
        take(piece)

        @pl.when(jnp.logical_and(here, quad == 0))
        def _():
            send_piece(piece, z + QUAD, far_ssem)

        return 0

    lax.fori_loop(QUAD, jnp.where(quad == 2, BLOCK, QUAD), send_across, 0)
    lax.fori_loop(z + 1, before_high, near_send, 0)
    lax.fori_loop(1, REACH, near_take, 0)

    soon = jnp.where(jnp.logical_and(early, z >= SOON), QUAD, 0)
    lax.fori_loop(0, soon, across_send, 0)

    for load in loads[7:11]:
        load.wait()
    pltpu.make_async_copy(msa_recv, msa_recv, msa_rsem).wait()
    items = jnp.concatenate(unpack_halves(msa_recv[...]), axis=1).astype(BF16)
    queries = (dot(items, wq[...]) * HEAD_SIZE ** (-0.5)).astype(BF16)
    keys = dot(items, wk[...]).astype(BF16)
    values = dot(items, wv[...]).astype(BF16)
    gates = jax.nn.sigmoid(dot(items, wg[...]))
    head = lax.div(iota((TOKENS, WIDTH), 1), HEAD_SIZE)
    zero = jnp.zeros((TOKENS, WIDTH), BF16)
    one = jnp.ones((TOKENS, WIDTH), BF16)
    queries_by_head = jnp.concatenate(
        [jnp.where(head == h, queries, zero) for h in range(HEADS)], axis=0
    )
    values_by_head = jnp.concatenate(
        [jnp.where(head == h, values, zero) for h in range(HEADS)], axis=0
    )
    ones_by_head = jnp.concatenate([jnp.where(head == h, one, zero) for h in range(HEADS)], axis=0)
    scores = dot_t(queries_by_head, keys) + (keep - 1.0) * 1e9
    weights = jnp.exp(scores - jnp.max(scores, axis=-1, keepdims=True)).astype(BF16)
    weights = jnp.concatenate(
        [weights[h * TOKENS : (h + 1) * TOKENS] for h in range(HEADS)], axis=1
    )
    mixed = dot(weights, values_by_head) / dot(weights, ones_by_head)
    attended = (mixed * gates).astype(BF16)
    loads[11].wait()
    loads[12].wait()
    upd_send[...] = pack_halves(dot(attended, wo[...]) + bo[...])

    relay(REACH)
    relay(-REACH)
    lax.fori_loop(before_high, reach_high, near_send, 0)
    lax.fori_loop(soon, jnp.where(quad == 1, BLOCK, 0), across_send, 0)
    send_rows(upd_send, upd_recv, upd_ssem, upd_rsem)
    for there in partners:
        pltpu.make_async_remote_copy(
            src_ref=lbuf.at[q],
            dst_ref=lbuf.at[q],
            send_sem=l_ssem,
            recv_sem=l_rsem,
            device_id=(d, there),
            device_id_type=MESH,
        ).start()
    lax.fori_loop(before + 1, BLOCK, near_take, 0)
    lax.fori_loop(0, jnp.where(quad == 0, BLOCK, 0), across_send, 0)
    lax.fori_loop(0, BLOCK, across_take, 0)

    pltpu.make_async_copy(upd_recv, upd_recv, upd_rsem).wait()
    by_row = (col == lax.rem(row, GROUPS) * ROWS + lax.div(row, GROUPS)).astype(F32).astype(BF16)
    update = jnp.concatenate(unpack_halves(upd_recv[...]), axis=1).astype(BF16)
    column_out[...] = dot(by_row, update).astype(BF16).reshape(ROWS, GROUPS, WIDTH)

    sent(lbuf.at[some], l_rsem)
    gap = jnp.zeros((GROUPS, ROWS, LANES), F32)
    lefts = []
    for side in range(2):
        parts = []
        for a in range(2):
            for tile in unpack_halves(lbuf[:, a]):
                rows = [tile.reshape(GROUPS, ROWS, LANES), gap]
                parts.append(
                    jnp.concatenate(rows[::-1] if side else rows, axis=1)
                    .reshape(2 * TOKENS, LANES)
                    .T
                )
        lefts.append(
            jnp.concatenate(parts, axis=0).astype(BF16).reshape(8, 4, GROUPS, 2 * TOKENS)
        )
    loads[13].wait()
    loads[14].wait()
    kept = jnp.sum(keep)

    for half in range(2):
        pltpu.make_async_copy(rbuf.at[half], rbuf.at[half], r_rsem.at[half]).wait()
    right = jnp.concatenate(
        [rbuf[half, :, a].reshape(2 * TOKENS, LANES) for half in range(2) for a in range(2)], axis=1
    )

    products = []
    for a in range(4):
        turned = [
            right[:, LANES * t : LANES * (t + 1)]
            if a == 0
            else pltpu.roll(right[:, LANES * t : LANES * (t + 1)], FACTORS * a, 1)
            for t in range(4)
        ]
        turned = jnp.concatenate(turned, axis=1)
        products.append(
            [
                dot(lefts[side][:, a].reshape(TOKENS, 2 * TOKENS), turned)
                .astype(BF16)
                .reshape(8, GROUPS, 4 * LANES)
                for side in range(2)
            ]
        )

    block = lax.div(iota((GROUPS, LANES), 1), FACTORS)
    odd, high = lax.rem(block, 2) == 1, block >= 2
    flat = [[[None] * 8 for _ in range(8)] for _ in range(4)]
    for t in range(4):
        for side in range(2):
            for c in range(8):
                v = [products[a][side][c, :, LANES * t : LANES * (t + 1)] for a in range(4)]
                even_up, even_down = jnp.where(high, v[2], v[0]), jnp.where(high, v[0], v[2])
                odd_up, odd_down = jnp.where(high, v[3], v[1]), jnp.where(high, v[1], v[3])
                place = 2 * t + side
                flat[0][place][c] = jnp.where(odd, odd_up, even_up)
                flat[1][place][c] = jnp.where(odd, even_up, odd_down)
                flat[2][place][c] = jnp.where(odd, odd_down, even_down)
                flat[3][place][c] = jnp.where(odd, even_down, odd_up)
    couple = wz[...].reshape(8, 4, FACTORS, C_Z)
    for b in range(4):
        mixing = jnp.concatenate(
            [couple[c, (g - b) % 4] for c in range(8) for g in range(4)], axis=0
        )
        sums = dot(
            jnp.concatenate([jnp.concatenate(r, axis=1) for r in flat[b]], axis=0), mixing
        )
        for place in range(8):
            total[pl.ds(4 * place + b, GROUPS, stride=2 * GROUPS), :] = sums[
                GROUPS * place : GROUPS * (place + 1)
            ]
    pair_out[...] = (total[...] / kept + bz[...]).astype(BF16).reshape(GROUPS, 2 * GROUPS, C_Z)

    sent(lbuf.at[some], l_ssem)
    sent(msa_send.at[some], msa_ssem)
    sent(upd_send.at[some], upd_ssem)

    @pl.when(quad == 3)
    def _():
        sent(zbuf.at[pl.ds(0, QUAD)], across_ssem)

    @pl.when(quad != 3)
    def _():
        sent(zbuf.at[pl.ds(0, BLOCK)], across_ssem)

    @pl.when(quad == 0)
    def _():
        sent(zbuf.at[pl.ds(0, QUAD)], far_ssem)

    def near_sent(there, _):
        @pl.when(there != z)
        def _():
            sent(zbuf.at[0], near_ssem.at[there])

        return 0

    lax.fori_loop(reach_low, reach_high, near_sent, 0)
    for i in range(1, REACH):
        up = jnp.logical_and(z - REACH >= first, z + i < last)
        down = jnp.logical_and(z + REACH < last, z - i >= first)

        @pl.when(jnp.logical_and(jnp.logical_not(early), jnp.logical_or(up, down)))
        def _():
            sent(zbuf.at[0], relay_ssem.at[i])

    sent(zbuf, r_ssem)
    sent(zbuf.at[some], r_ssem)


def store(column, pair, column_out, pair_out, sem):
    copies = [
        pltpu.make_async_copy(pair, pair_out, sem.at[0]),
        pltpu.make_async_copy(column, column_out, sem.at[1]),
    ]
    for copy in copies:
        copy.start()
    for copy in copies:
        copy.wait()


def local(
    alignment_activity,
    existing_strand_flags,
    existing_position_flags,
    asking_vector_map,
    lookup_address_map,
    content_vector_map,
    sigmoid_switch_map,
    final_mixing_map,
    final_offset_vector,
    first_factor_map,
    first_factor_offset,
    second_factor_map,
    second_factor_offset,
    couple_mixing_map,
    couple_change_offset,
):
    args = (
        alignment_activity,
        existing_strand_flags.reshape(1, -1),
        existing_position_flags.reshape(1, -1),
        asking_vector_map,
        lookup_address_map,
        content_vector_map,
        sigmoid_switch_map,
        final_mixing_map,
        final_offset_vector.reshape(1, -1),
        first_factor_map.T,
        first_factor_offset.reshape(1, -1),
        second_factor_map.T,
        second_factor_offset.reshape(1, -1),
        couple_mixing_map,
        couple_change_offset.reshape(1, -1),
    )
    piece = (2 * ROWS, LANES)
    results = pl.pallas_call(
        kernel,
        out_shape=(
            jax.ShapeDtypeStruct((ROWS, GROUPS, WIDTH), BF16),
            jax.ShapeDtypeStruct((GROUPS, 2 * GROUPS, C_Z), BF16),
        ),
        in_specs=[pl.BlockSpec(memory_space=pl.ANY)] * len(args),
        out_specs=[pl.BlockSpec(memory_space=pltpu.VMEM)] * 2,
        scratch_shapes=[pltpu.VMEM(a.shape, a.dtype) for a in args]
        + [
            pltpu.VMEM((GROUPS, *piece), BF16),
            pltpu.VMEM((GROUPS, *piece), BF16),
            pltpu.VMEM((GROUPS, *piece), BF16),
            pltpu.VMEM((GROUPS, *piece), BF16),
            pltpu.VMEM((GROUPS, 2, *piece), BF16),
            pltpu.VMEM((GROUPS, 2, *piece), BF16),
            pltpu.VMEM((2, GROUPS, 2, *piece), BF16),
            pltpu.VMEM((2 * WIDTH, C_Z), F32),
            pltpu.SemaphoreType.DMA((len(args),)),
            pltpu.SemaphoreType.DMA,
            pltpu.SemaphoreType.DMA,
            pltpu.SemaphoreType.DMA,
            pltpu.SemaphoreType.DMA,
            pltpu.SemaphoreType.DMA,
            pltpu.SemaphoreType.DMA,
            pltpu.SemaphoreType.DMA,
            pltpu.SemaphoreType.DMA,
            pltpu.SemaphoreType.DMA((GROUPS,)),
            pltpu.SemaphoreType.DMA((REACH,)),
            pltpu.SemaphoreType.DMA((GROUPS,)),
            pltpu.SemaphoreType.DMA,
            pltpu.SemaphoreType.DMA((2,)),
            pltpu.SemaphoreType.REGULAR((GROUPS,)),
        ],
        compiler_params=pltpu.CompilerParams(
            collective_id=0, has_side_effects=True, vmem_limit_bytes=16 * 1024 * 1024
        ),
        name="column_attention_and_outer_mean",
    )(*[pltpu.with_memory_space_constraint(a, pltpu.HBM) for a in args])
    return pl.pallas_call(
        store,
        out_shape=tuple(jax.ShapeDtypeStruct(r.shape, r.dtype) for r in results),
        in_specs=[pl.BlockSpec(memory_space=pltpu.VMEM)] * 2,
        out_specs=[pl.BlockSpec(memory_space=pltpu.HBM)] * 2,
        scratch_shapes=[pltpu.SemaphoreType.DMA((2,))],
        compiler_params=pltpu.CompilerParams(vmem_limit_bytes=2 * 1024 * 1024),
        name="store_results",
    )(*[pltpu.with_memory_space_constraint(r, pltpu.VMEM) for r in results])


def solution(mesh):
    return jax.shard_map(
        local,
        mesh=mesh,
        in_specs=(P("pair", "dap", None),) + (P(),) * 14,
        out_specs=(P("pair", "dap", None), P("dap", "pair", None)),
        check_vma=False,
    )
```
